512 devices in a mesh: patch: 512 (over z, x, y, core).
Axes of the slice: x: 4, y: 8, z: 8, core: 2. Of those that a mesh axis runs over, the one named last changes fastest.
Arguments:
- inputs: bfloat16 [1536, 32, 32, 128], P('patch'), may hold values from -6 to 6
- cotangent: bfloat16 [1536, 32, 32, 128], P('patch'), may hold values from -6 to 6
- weights: bfloat16 [3, 3, 128, 128], replicated, may hold values from -0.1875 to 0.1875
- bias_vector: float32 [128], replicated, may hold values from -3 to 3
- neighbours: int32 [1536, 8], P('patch'), may hold values from 0 to 1535, as said below
- rotations: int32 [1536, 8], P('patch'), may hold values from 0 to 3
- corners: int32 [1536, 8], P('patch'), may hold values from 0 to 1, as said below
Outputs:
- outputs: bfloat16 [1536, 32, 32, 128], P('patch')
- input_grad: bfloat16 [1536, 32, 32, 128], P('patch')
- weight_grad: float32 [3, 3, 128, 128], replicated
- bias_grad: float32 [128], replicated
The draws below stay inside these ranges and needn't reach their ends.
Inputs may be any that keep to these rules, and one draw needn't show every extreme that they name: `neighbours`: the neighbour of a patch on device d lies on a device d + o (modulo the device count) with |o| <= 2; offsets 2 and -2 both occur. `corners`: the four side directions are always 1.
All inputs are finite; a program needn't handle non-finite values.
Results may differ from the reference program's by a relative error of at most 0.0035.
Values may be sent and summed in bfloat16 or wider, within the bound.
A program may use at most 64 MiB of HBM per device.

```python
import math
import jax
import jax.numpy as jnp
from jax import lax

CH = 128
SIDE = 32
REACH = 2
PATCH_DEV = 3
PATCHES = 1536


def draw_neighbours(key, part):
    key_off = jax.random.fold_in(key, 11)
    key_pos = jax.random.fold_in(key, 12)
    devices_all = PATCHES // PATCH_DEV
    rows = jnp.arange(PATCHES)
    owners = rows // PATCH_DEV
    offset = jax.random.randint(key_off, (PATCHES, 8), -REACH, REACH + 1)
    offset = offset.at[0, 1].set(REACH).at[0, 6].set(-REACH)
    offset = offset.at[0, 0].set(-1).at[PATCH_DEV, 3].set(-1)
    within = jax.random.randint(key_pos, (PATCHES, 8), 0, PATCH_DEV)
    within = within.at[0, 0].set(PATCH_DEV - 1).at[PATCH_DEV, 3].set(0)
    target = (owners[:, None] + offset) % devices_all
    return (target * PATCH_DEV + within).astype(jnp.int32)


def draw_corners(key, part):
    key_flag = jax.random.fold_in(key, 21)
    values = jax.random.randint(key_flag, (PATCHES, 8), 0, 4)
    diagonal = jnp.array([1, 0, 1, 0, 0, 1, 0, 1], dtype=jnp.int32)[None, :]
    flags = jnp.where(values > 0, 1, 0)
    flags = jnp.where(diagonal > 0, flags, 1)
    flags = flags.at[0, 0].set(0).at[0, 2].set(1)
    return flags.astype(jnp.int32)


def set_ends(values, own_key, least, largest):
    extent = values.shape
    place = [jax.random.randint(jax.random.fold_in(own_key, axis), (), 0, extent[axis]) for axis in range(len(extent))]
    values = values.at[tuple(place)].set(least)
    longest = extent.index(max(extent))
    place[longest] = (place[longest] + 1) % extent[longest]
    return values.at[tuple(place)].set(largest)


def block_scale(stream_key, extent, cuts, low, largest):
    level, own = 1.0, jax.random.fold_in(stream_key, 6)
    for dim, blocks in cuts:
        steps = jnp.exp(jax.random.uniform(jax.random.fold_in(own, dim), (blocks,), jnp.float32, low / len(cuts), largest / len(cuts)))
        level = level * jnp.repeat(steps, extent[dim] // blocks).reshape([-1 if axis == dim else 1 for axis in range(len(extent))])
    return level


def bell_draw(key, dims, spread, most, cuts=(), kind=jnp.bfloat16):
    drawn = spread * jax.random.normal(key, dims, jnp.float32)
    if cuts:
        drawn = drawn * block_scale(key, dims, cuts, -0.22, 0.18)
    return jnp.clip(drawn, -most, most).astype(kind)


def setup_inputs(seed: int = 0) -> dict:
    streams_of = jax.random.split(jax.random.key(seed), 8)
    inputs = bell_draw(streams_of[0], (PATCHES, SIDE, SIDE, CH), 1.0, 6.0, ((0, 512),))
    cotangent = bell_draw(streams_of[1], (PATCHES, SIDE, SIDE, CH), 1.0, 6.0, ((0, 512),))
    weights = bell_draw(streams_of[2], (3, 3, CH, CH), (9 * CH) ** -0.5, 0.1875)
    bias_vector = bell_draw(streams_of[3], (CH,), 0.5, 3.0, (), jnp.float32)
    neighbours = draw_neighbours(jax.random.fold_in(streams_of[7], 71), 0)
    rotations = set_ends(jax.random.randint(streams_of[5], (PATCHES, 8), 0, 4), jax.random.fold_in(streams_of[5], 1), 0, 3).astype(jnp.int32)
    corners = draw_corners(jax.random.fold_in(streams_of[7], 71), 0)
    return dict(inputs=inputs, cotangent=cotangent, weights=weights, bias_vector=bias_vector, neighbours=neighbours, rotations=rotations, corners=corners)


DIRECTIONS = ((-1, -1), (-1, 0), (-1, 1), (0, -1), (0, 1), (1, -1), (1, 0), (1, 1))

def aligned_span(step, length):
    if step < 0:
        return slice(length - 2, length)
    if step == 0:
        return slice(0, length)
    return slice(0, 2)

def edge_strips(patches):
    length = patches.shape[1]
    upper = patches[:, 0:2]
    lower = patches[:, length - 2:]
    rows = jnp.arange(length)
    inside = ((rows >= 2) & (rows < length - 2))[None, None, :, None]
    left_cols = jnp.swapaxes(patches[:, :, 0:2], 1, 2)
    left_cols = jnp.where(inside, left_cols, jnp.zeros_like(left_cols))
    right_cols = jnp.swapaxes(patches[:, :, length - 2:], 1, 2)
    right_cols = jnp.where(inside, right_cols, jnp.zeros_like(right_cols))
    return jnp.stack([upper, lower, left_cols, right_cols], axis=1)

def edge_frame(strips):
    length = strips.shape[3]
    upper = strips[:, 0]
    lower = strips[:, 1]
    left_cols = jnp.swapaxes(strips[:, 2], 1, 2)[:, 2:length - 2]
    right_cols = jnp.swapaxes(strips[:, 3], 1, 2)[:, 2:length - 2]
    hollow = jnp.zeros((strips.shape[0], length - 4, length - 4, strips.shape[4]), strips.dtype)
    middle = jnp.concatenate([left_cols, hollow, right_cols], axis=2)
    return jnp.concatenate([upper, middle, lower], axis=1)

def rotate_frame(frames, quarter):
    turns = quarter[:, None, None, None]
    result = jnp.where(turns == 0, frames, jnp.zeros_like(frames))
    for k in range(1, 4):
        result = jnp.where(turns == k, jnp.rot90(frames, k, axes=(1, 2)), result)
    return result

def extend_patch(center, gathered, rotations, corners):
    pieces = {}
    for j, (row_step, col_step) in enumerate(DIRECTIONS):
        length = center.shape[1]
        aligned = rotate_frame(edge_frame(gathered[:, j]), rotations[:, j])
        region = aligned[:, aligned_span(row_step, length), aligned_span(col_step, length)]
        present = corners[:, j][:, None, None, None] > 0
        pieces[row_step, col_step] = jnp.where(present, region, jnp.zeros_like(region))
    upper = jnp.concatenate([pieces[-1, -1], pieces[-1, 0], pieces[-1, 1]], axis=2)
    middle = jnp.concatenate([pieces[0, -1], center, pieces[0, 1]], axis=2)
    lower = jnp.concatenate([pieces[1, -1], pieces[1, 0], pieces[1, 1]], axis=2)
    return jnp.concatenate([upper, middle, lower], axis=1)

def dilated_conv(extended, kernel):
    return lax.conv_general_dilated(extended, kernel, (1, 1), 'VALID', rhs_dilation=(2, 2), dimension_numbers=('NHWC', 'HWIO', 'NHWC'), precision=lax.Precision.HIGHEST, preferred_element_type=jnp.float32)

def reference(inputs, cotangent, weights, bias_vector, neighbours, rotations, corners):
    inputs_wide = inputs.astype(jnp.float32)
    weight_wide = weights.astype(jnp.float32)
    groups = jnp.arange(PATCHES).astype(jnp.int32).reshape(-1, PATCH_DEV)

    def forward(source, kernel, offsets):
        strips_all = edge_strips(source)

        def single(members):
            gathered = strips_all[neighbours[members]]
            extended = extend_patch(source[members], gathered, rotations[members], corners[members])
            return dilated_conv(extended, kernel) + offsets
        result = lax.map(jax.checkpoint(single), groups)
        return result.reshape(PATCHES, SIDE, SIDE, CH)
    result, pullback = jax.vjp(forward, inputs_wide, weight_wide, bias_vector)
    grad_in, grad_weight, grad_bias = pullback(cotangent.astype(jnp.float32))
    factor = 1.0 / (SIDE * math.sqrt(PATCHES))
    return (result.astype(jnp.bfloat16), grad_in.astype(jnp.bfloat16), grad_weight * factor, grad_bias * factor)
```

```python
import functools
import math

import jax
import jax.numpy as jnp
from jax import lax
from jax.experimental import pallas as pl
from jax.experimental.pallas import tpu as pltpu
from jax.sharding import PartitionSpec as P

REACH = 2
MESH = pl.DeviceIdType.MESH
BF = jnp.bfloat16
F32 = jnp.float32
SIDE_TABLE = (
    ((0, 0), (3, 1), (1, 3), (2, 2)),
    ((1, 0), (2, 1), (0, 3), (3, 2)),
    ((2, 0), (0, 2), (3, 3), (1, 1)),
    ((3, 0), (1, 2), (2, 3), (0, 1)),
)
WANTED = (1, 1, 1, 3, 2, 0, 0, 0)
TORUS = {512: (8, 4, 8), 16: (2, 2, 2)}


def pick(k, values):
    out = jnp.int32(values[3])
    for i in (2, 1, 0):
        out = jnp.where(k == i, jnp.int32(values[i]), out)
    return out


def side_scalars(j, nb, rot, me, count, here):
    owner = nb // here
    off = lax.rem(owner - me + REACH + count, count)
    place = jnp.minimum(off, 2 * REACH) * here + (nb - owner * here)
    table = SIDE_TABLE[WANTED[j]]
    slot = pick(rot, [table[k][0] for k in range(4)])
    c1 = pick(rot, [table[k][1] & 1 for k in range(4)])
    c2 = pick(rot, [table[k][1] >> 1 for k in range(4)])
    return place * 4 + slot, c1, c2


def onehot(target, width):
    rows = target.shape[0]
    lanes = lax.broadcasted_iota(jnp.int32, (rows, width), 1)
    return jnp.where(lanes == target, 1.0, 0.0).astype(BF)


def rows_iota(rows):
    return lax.broadcasted_iota(jnp.int32, (rows, 1), 0)


def flip(c, x, last):
    return last * c + (1 - 2 * c) * x


def dot(a, b):
    return jnp.dot(a, b, preferred_element_type=F32)


def prepare_kernel(
    count, nb, rot, cor, inp, cot, wt, strips, terms, center, acc, zl, zr, cpad
):
    me = lax.axis_index("patch")
    here = inp.shape[0]
    acc[...] = jnp.zeros_like(acc)
    cpad[0:4] = jnp.zeros((4, 32, 128), BF)
    cpad[36:40] = jnp.zeros((4, 32, 128), BF)
    r64 = rows_iota(64)
    depth, along = r64 // 32, lax.rem(r64, 32)
    cols = lax.broadcasted_iota(jnp.int32, (6, 32, 128), 1)

    def patch(p, carry):
        strips[p * 4] = inp[p, 0:2].reshape(64, 128)
        strips[p * 4 + 1] = inp[p, 30:32].reshape(64, 128)
        left = inp[p, :, 0:16, :].reshape(512, 128)
        strips[p * 4 + 2] = dot(onehot(along * 16 + depth, 512), left).astype(BF)
        right = inp[p, :, 16:32, :].reshape(512, 128)
        strips[p * 4 + 3] = dot(onehot(along * 16 + depth + 14, 512), right).astype(BF)
        cpad[4:36] = cot[p]

        def chunk(n, c):
            y0 = n * 6
            lhs = jnp.concatenate(
                [cpad[pl.ds(y0 + 4 - 2 * a, 6)].reshape(192, 128) for a in range(3)],
                axis=1,
            )
            z = dot(lhs, wt[...])
            z0 = z[:, 0:128].reshape(6, 32, 128)
            z1 = z[:, 128:256].reshape(6, 32, 128)
            z2 = z[:, 256:384].reshape(6, 32, 128)
            zl[pl.ds(y0, 6)] = z0[:, 0:16].astype(BF)
            zr[pl.ds(y0, 6)] = z2[:, 16:32].astype(BF)
            total = z1 + jnp.where(cols < 30, pltpu.roll(z0, 30, 1), 0.0)
            total = total + jnp.where(cols >= 2, pltpu.roll(z2, 2, 1), 0.0)
            center[p, pl.ds(y0, 6)] = total
            return c

        lax.fori_loop(0, 6, chunk, 0)

        def back(j, target_of, block):
            row, c1, c2 = side_scalars(j, nb[p, j], rot[p, j], me, count, here)
            target = target_of(flip(c1, depth, 1), flip(c2, along, 31))
            target = jnp.where(cor[p, j] > 0, target, -1)
            acc[row] = acc[row] + dot(onehot(target, block.shape[0]), block)

        def last_two(step, q):
            return jnp.where(q >= 30, step + q - 30, -1)

        def first_two(step, q):
            return jnp.where(q < 2, step + 14 + q, -1)

        for base, rows in ((0, slice(0, 2)), (5, slice(34, 36))):
            mid = center[p, rows].reshape(64, 128).astype(BF)
            back(base, lambda r, q: last_two(16 * r, q), zl[rows].reshape(32, 128))
            back(base + 1, lambda r, q: 32 * r + q, mid)
            back(base + 2, lambda r, q: first_two(16 * r, q), zr[rows].reshape(32, 128))
        back(3, lambda c, i: 16 * i + c, zl[2:34].reshape(512, 128))
        back(4, lambda c, i: 16 * i + 14 + c, zr[2:34].reshape(512, 128))
        return carry

    lax.fori_loop(0, here, patch, 0)

    def narrow(n, c):
        terms[n] = acc[n].astype(BF)
        return c

    lax.fori_loop(0, terms.shape[0], narrow, 0)


def main_kernel(
    sizes,
    factor,
    nb,
    rot,
    cor,
    inp,
    cot,
    w,
    bias,
    strips,
    terms,
    center,
    out,
    ingrad,
    wgrad,
    bgrad,
    pool,
    arr,
    xs,
    cpad,
    wacc,
    wloc,
    core_out,
    core_in,
    y_out,
    y_in,
    z_out,
    z_in,
    x_all,
    z_all,
    fin,
    s_edge,
    r_edge,
    s_term,
    r_term,
    s_core,
    r_core,
    s_y,
    r_y,
    s_z,
    r_z,
    s_x,
    r_x,
    s_za,
    r_za,
    s_ya,
    r_ya,
    s_ca,
    r_ca,
):
    nz, nx, ny = sizes
    count = nz * nx * ny * 2
    me = lax.axis_index("patch")
    here = inp.shape[0]
    core = lax.rem(me, 2)
    y = lax.rem(me // 2, ny)
    x = lax.rem(me // (2 * ny), nx)
    z = me // (2 * ny * nx)
    mate = me + 1 - 2 * core
    block = here * 4
    zr, yr = wloc.shape[1] // nz, wloc.shape[1]

    def y_peer(k):
        yk = lax.rem(y + k, ny)
        return yk, me + 2 * (yk - y)

    def z_peer(k):
        zk = lax.rem(z + k, nz)
        return zk, me + 2 * ny * nx * (zk - z)

    def x_peer(k):
        xk = lax.rem(x + k, nx)
        return xk, me + 2 * ny * (xk - x)

    def near(o):
        return lax.rem(me + o + count, count)

    def copy(src, dst, send, recv, to):
        return pltpu.make_async_remote_copy(
            src_ref=src,
            dst_ref=dst,
            send_sem=send,
            recv_sem=recv,
            device_id=(to,),
            device_id_type=MESH,
        )

    barrier = pltpu.get_barrier_semaphore()
    peers = [mate]
    peers += [y_peer(k)[1] for k in range(1, ny)]
    peers += [z_peer(k)[1] for k in range(1, nz)]
    peers += [x_peer(k)[1] for k in range(1, nx)]
    peers += [near(o) for o in (-2, -1, 1, 2)]
    for peer in peers:
        pl.semaphore_signal(barrier, inc=1, device_id=(peer,), device_id_type=MESH)
    pl.semaphore_wait(barrier, len(peers))

    edges, backs = [], []
    for n, o in enumerate((-2, -1, 1, 2)):
        edges.append(
            copy(
                strips,
                pool.at[pl.ds((REACH - o) * block, block)],
                s_edge.at[n],
                r_edge.at[n],
                near(o),
            )
        )
        edges[-1].start()
    for n, o in enumerate((-2, -1, 1, 2)):
        backs.append(
            copy(
                terms.at[pl.ds((REACH + o) * block, block)],
                arr.at[n],
                s_term.at[n],
                r_term.at[n],
                near(o),
            )
        )
        backs[-1].start()
    pool[REACH * block : (REACH + 1) * block] = strips[...]

    cols = lax.broadcasted_iota(jnp.int32, (32, 32, 128), 1)

    def middle(p, total):
        here_in = inp[p]
        wide = here_in.astype(F32)
        xs[p, 2:34, :, 128:256] = here_in
        ahead = jnp.where(cols >= 2, pltpu.roll(wide, 2, 1), 0.0)
        xs[p, 2:34, :, 0:128] = ahead.astype(BF)
        behind = jnp.where(cols < 30, pltpu.roll(wide, 30, 1), 0.0)
        xs[p, 2:34, :, 256:384] = behind.astype(BF)
        cpad[p, 0:4] = jnp.zeros((4, 32, 128), BF)
        cpad[p, 36:40] = jnp.zeros((4, 32, 128), BF)
        here_cot = cot[p]
        cpad[p, 4:36] = here_cot
        return total + here_cot.astype(F32).reshape(128, 8, 128).sum(axis=0)

    bias8 = lax.fori_loop(0, here, middle, jnp.zeros((8, 128), F32))
    bias_here = jnp.sum(bias8, axis=0, keepdims=True)
    for c in edges:
        c.wait_recv()

    r192 = rows_iota(192)
    tap, depth, along = r192 // 64, lax.rem(r192 // 32, 2), lax.rem(r192, 32)
    at = 2 * tap + along
    r512 = rows_iota(512)
    line, place = r512 // 16, lax.rem(r512, 16)

    def halo(p, carry):
        def info(j):
            row, c1, c2 = side_scalars(j, nb[p, j], rot[p, j], me, count, here)
            return pool[row], c1, c2, cor[p, j] > 0

        for base, first in ((0, 0), (5, 34)):
            made = jnp.zeros((192, 128), F32)
            for j, q, inside in (
                (base, 30 + at, at < 2),
                (base + 1, at - 2, (at >= 2) & (at < 34)),
                (base + 2, at - 34, at >= 34),
            ):
                strip, c1, c2, present = info(j)
                target = 32 * flip(c1, depth, 1) + flip(c2, q, 31)
                target = jnp.where(inside & present, target, -1)
                made = made + dot(onehot(target, 64), strip)
            made = made.astype(BF)
            for b in range(3):
                piece = made[64 * b : 64 * b + 64].reshape(2, 32, 128)
                xs[p, first : first + 2, :, 128 * b : 128 * b + 128] = piece
        strip, c1, c2, present = info(3)
        target = 32 * flip(c1, place, 1) + flip(c2, line, 31)
        target = jnp.where((place < 2) & present, target, -1)
        made = dot(onehot(target, 64), strip).reshape(32, 16, 128)
        old = xs[p, 2:34, 0:16, 0:128].astype(F32)
        xs[p, 2:34, 0:16, 0:128] = (old + made).astype(BF)
        strip, c1, c2, present = info(4)
        target = 32 * flip(c1, place - 14, 1) + flip(c2, line, 31)
        target = jnp.where((place >= 14) & present, target, -1)
        made = dot(onehot(target, 64), strip).reshape(32, 16, 128)
        old = xs[p, 2:34, 16:32, 256:384].astype(F32)
        xs[p, 2:34, 16:32, 256:384] = (old + made).astype(BF)
        return carry

    lax.fori_loop(0, here, halo, 0)

    wacc[...] = jnp.zeros_like(wacc)

    def outer(n, carry):
        p, y0 = n // 3, lax.rem(n, 3) * 12
        lhs = xs[p, pl.ds(y0, 12)].reshape(384, 384)
        rhs = jnp.concatenate(
            [cpad[p, pl.ds(y0 + 4 - 2 * a, 12)].reshape(384, 128) for a in range(3)],
            axis=1,
        )
        wacc[...] += lax.dot_general(
            lhs, rhs, (((0,), (0,)), ((), ())), preferred_element_type=F32
        )
        return carry

    lax.fori_loop(0, here * 3, outer, 0)

    taps = [wacc[128 * b : 128 * b + 128, 128 * a : 128 * a + 128] for a in range(3) for b in range(3)]
    for s in range(2 * ny):
        lo, hi = s * yr, (s + 1) * yr
        while lo < hi:
            t = lo // 128
            end = min(hi, (t + 1) * 128)
            wloc[s, lo - s * yr : end - s * yr] = taps[t][lo - 128 * t : end - 128 * t]
            lo = end

    row8 = lax.broadcasted_iota(jnp.int32, (8, 128), 0)

    def bias_rows(b):
        top = b.astype(BF).astype(F32)
        return jnp.where(row8 == 0, top, jnp.where(row8 == 1, b - top, 0.0))

    def bias_of(rows):
        return rows[0:1] + rows[1:2]

    mine = bias_rows(bias_here)

    def to_mate(s, carry):
        core_out[s, 0:yr] = wloc[(1 - core) * ny + s].astype(BF)
        core_out[s, yr : yr + 8] = mine.astype(BF)
        return carry

    lax.fori_loop(0, ny, to_mate, 0)
    swap = copy(core_out, core_in, s_core, r_core, mate)
    swap.start()

    def conv(n, carry):
        p, i0 = n // 4, lax.rem(n, 4) * 8
        lhs = jnp.concatenate(
            [xs[p, pl.ds(i0 + 2 * a, 8)].reshape(256, 384) for a in range(3)], axis=1
        )
        out[p, pl.ds(i0, 8)] = (dot(lhs, w[...]) + bias[...]).astype(BF).reshape(8, 32, 128)
        return carry

    lax.fori_loop(0, 2, conv, 0)
    swap.wait_recv()

    def pair(s):
        data = wloc[core * ny + s] + core_in[s, 0:yr].astype(F32)
        return data, mine + core_in[s, yr : yr + 8].astype(F32)

    def to_line(s, carry):
        data, extra = pair(s)
        y_out[s, 0:yr] = data.astype(BF)
        y_out[s, yr : yr + 8] = bias_rows(bias_of(extra)).astype(BF)
        return carry

    lax.fori_loop(0, ny, to_line, 0)

    def y_reduce(k):
        yk, peer = y_peer(k)
        return copy(y_out.at[yk], y_in.at[k - 1], s_y.at[k - 1], r_y.at[k - 1], peer)

    for k in range(1, ny):
        y_reduce(k).start()
    lax.fori_loop(2, 8, conv, 0)
    data, extra = pair(y)
    for k in range(1, ny):
        y_reduce(k).wait_recv()
        data = data + y_in[k - 1, 0:yr].astype(F32)
        extra = extra + y_in[k - 1, yr : yr + 8].astype(F32)
    total_bias = bias_of(extra)
    z_out[...] = jnp.zeros_like(z_out)
    for zz in range(nz):
        z_out[zz, 0:zr] = data[zz * zr : (zz + 1) * zr]
        z_out[zz, zr : zr + 1] = total_bias

    def z_reduce(k):
        zk, peer = z_peer(k)
        return copy(z_out.at[zk], z_in.at[k - 1], s_z.at[k - 1], r_z.at[k - 1], peer)

    for k in range(1, nz):
        z_reduce(k).start()
    lax.fori_loop(8, 4 * here, conv, 0)
    data = z_out[z]
    for k in range(1, nz):
        z_reduce(k).wait_recv()
        data = data + z_in[k - 1]
    x_all[x] = data

    def x_gather(k):
        return copy(x_all.at[x], x_all.at[x], s_x.at[k - 1], r_x.at[k - 1], x_peer(k)[1])

    for k in range(1, nx):
        x_gather(k).start()
    for c in backs:
        c.wait_recv()

    def finish(p, carry):
        def arrived(slot):
            total = terms[REACH * block + p * 4 + slot].astype(F32)
            for n in range(4):
                total = total + arr[n, p * 4 + slot].astype(F32)
            return total.reshape(2, 32, 128)

        def columns(slot, shift):
            stack = [terms[REACH * block + p * 4 + slot]]
            stack += [arr[n, p * 4 + slot] for n in range(4)]
            spot = place - shift
            target = jnp.where((spot >= 0) & (spot < 2), 32 * spot + line, -1)
            spread = onehot(target, 64)
            made = jnp.zeros((512, 128), F32)
            for piece in stack:
                made = made + dot(spread, piece)
            return made.reshape(32, 16, 128)

        center[p, 2:34, 0:16] = center[p, 2:34, 0:16] + columns(2, 0)
        center[p, 2:34, 16:32] = center[p, 2:34, 16:32] + columns(3, 14)
        center[p, 2:4] = center[p, 2:4] + arrived(0)
        center[p, 32:34] = center[p, 32:34] + arrived(1)
        ingrad[p] = center[p, 2:34].astype(BF)
        return carry

    lax.fori_loop(0, here, finish, 0)
    for k in range(1, nx):
        x_gather(k).wait_recv()
    data = x_all[0]
    for n in range(1, nx):
        data = data + x_all[n]
    data = data * factor
    row_z = lax.broadcasted_iota(jnp.int32, data.shape, 0)
    b = data[zr : zr + 1]
    top = b.astype(BF).astype(F32)
    data = jnp.where(row_z == zr, top, jnp.where(row_z == zr + 1, b - top, data))
    z_all[z] = data.astype(BF)

    def z_gather(k):
        return copy(z_all.at[z], z_all.at[z], s_za.at[k - 1], r_za.at[k - 1], z_peer(k)[1])

    for k in range(1, nz):
        z_gather(k).start()
    for k in range(1, nz):
        z_gather(k).wait_recv()
    pieces = [z_all[zz].astype(F32) for zz in range(nz)]
    slab = jnp.concatenate([piece[0:zr] for piece in pieces], axis=0)
    spot = core * ny + y
    fin[spot, 0:yr] = slab.astype(BF)
    tail = pieces[0][zr : zr + 2]
    fin[spot, yr : yr + 8] = jnp.where(
        row8 == 0, tail[0:1], jnp.where(row8 == 1, tail[1:2], 0.0)
    ).astype(BF)

    def y_gather(k):
        return copy(fin.at[spot], fin.at[spot], s_ya.at[k - 1], r_ya.at[k - 1], y_peer(k)[1])

    def c_gather(k):
        at_y = core * ny + lax.rem(y - k + ny, ny)
        return copy(fin.at[at_y], fin.at[at_y], s_ca.at[k], r_ca.at[k], mate)

    for k in range(1, ny):
        y_gather(k).start()
    c_gather(0).start()
    for k in range(1, ny):
        y_gather(k).wait_recv()
        c_gather(k).start()
    for k in range(ny):
        c_gather(k).wait_recv()
    for s in range(2 * ny):
        wgrad[s * yr : (s + 1) * yr] = fin[s, 0:yr].astype(F32)
    tail = fin[0, yr : yr + 8].astype(F32)
    bgrad[...] = jnp.broadcast_to(bias_of(tail), bgrad.shape)

    for c in edges + backs + [swap]:
        c.wait_send()
    for k in range(1, ny):
        y_reduce(k).wait_send()
        y_gather(k).wait_send()
    for k in range(1, nz):
        z_reduce(k).wait_send()
        z_gather(k).wait_send()
    for k in range(1, nx):
        x_gather(k).wait_send()
    for k in range(ny):
        c_gather(k).wait_send()


def body(count, inputs, cotangent, weights, bias_vector, neighbours, rotations, corners):
    here, length, _, chans = inputs.shape
    sizes = TORUS[count]
    nz, nx, ny = sizes
    factor = 1.0 / (length * math.sqrt(here * count))
    block = here * 4
    smem = pl.BlockSpec(memory_space=pltpu.SMEM)
    vmem = pl.BlockSpec(memory_space=pltpu.VMEM)
    dma = pltpu.SemaphoreType.DMA
    turned = weights.transpose(0, 3, 1, 2).reshape(3 * chans, 3 * chans)
    strips, terms, center = pl.pallas_call(
        functools.partial(prepare_kernel, count),
        out_shape=(
            jax.ShapeDtypeStruct((block, 64, chans), BF),
            jax.ShapeDtypeStruct((5 * block, 64, chans), BF),
            jax.ShapeDtypeStruct((here, 36, 32, chans), F32),
        ),
        in_specs=[smem] * 3 + [vmem] * 3,
        out_specs=(vmem,) * 3,
        scratch_shapes=[
            pltpu.VMEM((5 * block, 64, chans), F32),
            pltpu.VMEM((36, 16, chans), BF),
            pltpu.VMEM((36, 16, chans), BF),
            pltpu.VMEM((40, 32, chans), BF),
        ],
        compiler_params=pltpu.CompilerParams(vmem_limit_bytes=40 * 2**20),
    )(neighbours, rotations, corners, inputs, cotangent, turned)

    yr = 9 * chans // (2 * ny)
    zr = yr // nz
    zpad = -(-(zr + 2) // 16) * 16
    outputs, input_grad, weight_grad, bias_grad = pl.pallas_call(
        functools.partial(main_kernel, sizes, factor),
        out_shape=(
            jax.ShapeDtypeStruct(inputs.shape, BF),
            jax.ShapeDtypeStruct(inputs.shape, BF),
            jax.ShapeDtypeStruct((9 * chans, chans), F32),
            jax.ShapeDtypeStruct((8, chans), F32),
        ),
        in_specs=[smem] * 3 + [vmem] * 7,
        out_specs=(vmem,) * 4,
        scratch_shapes=[
            pltpu.VMEM((5 * block, 64, chans), BF),
            pltpu.VMEM((4, block, 64, chans), BF),
            pltpu.VMEM((here, 36, 32, 3 * chans), BF),
            pltpu.VMEM((here, 40, 32, chans), BF),
            pltpu.VMEM((3 * chans, 3 * chans), F32),
            pltpu.VMEM((2 * ny, yr, chans), F32),
            pltpu.VMEM((ny, yr + 8, chans), BF),
            pltpu.VMEM((ny, yr + 8, chans), BF),
            pltpu.VMEM((ny, yr + 8, chans), BF),
            pltpu.VMEM((ny - 1, yr + 8, chans), BF),
            pltpu.VMEM((nz, zpad, chans), F32),
            pltpu.VMEM((nz - 1, zpad, chans), F32),
            pltpu.VMEM((nx, zpad, chans), F32),
            pltpu.VMEM((nz, zpad, chans), BF),
            pltpu.VMEM((2 * ny, yr + 8, chans), BF),
            dma((4,)),
            dma((4,)),
            dma((4,)),
            dma((4,)),
            dma,
            dma,
            dma((ny - 1,)),
            dma((ny - 1,)),
            dma((nz - 1,)),
            dma((nz - 1,)),
            dma((nx - 1,)),
            dma((nx - 1,)),
            dma((nz - 1,)),
            dma((nz - 1,)),
            dma((ny - 1,)),
            dma((ny - 1,)),
            dma((ny,)),
            dma((ny,)),
        ],
        compiler_params=pltpu.CompilerParams(
            collective_id=0, has_side_effects=True, vmem_limit_bytes=48 * 2**20
        ),
    )(
        neighbours,
        rotations,
        corners,
        inputs,
        cotangent,
        weights.reshape(9 * chans, chans),
        bias_vector.reshape(1, chans),
        strips,
        terms,
        center,
    )
    return (
        outputs,
        input_grad,
        weight_grad.reshape(3, 3, chans, chans),
        bias_grad[0],
    )


def solution(mesh):
    in_specs = (
        P("patch", None, None, None),
        P("patch", None, None, None),
        P(),
        P(),
        P("patch", None),
        P("patch", None),
        P("patch", None),
    )
    out_specs = (P("patch", None, None, None), P("patch", None, None, None), P(), P())
    return jax.shard_map(
        functools.partial(body, mesh.shape["patch"]),
        mesh=mesh,
        in_specs=in_specs,
        out_specs=out_specs,
        check_vma=False,
    )
```

```python
import functools
import math

import jax
import jax.numpy as jnp
from jax import lax
from jax.experimental import pallas as pl
from jax.experimental.pallas import tpu as pltpu
from jax.sharding import PartitionSpec as P

REACH = 2
NEAR = (-2, -1, 1, 2)
MESH = pl.DeviceIdType.MESH
BF = jnp.bfloat16
F32 = jnp.float32
SIDE_TABLE = (
    ((0, 0), (3, 1), (1, 3), (2, 2)),
    ((1, 0), (2, 1), (0, 3), (3, 2)),
    ((2, 0), (0, 2), (3, 3), (1, 1)),
    ((3, 0), (1, 2), (2, 3), (0, 1)),
)
WANTED = (1, 1, 1, 3, 2, 0, 0, 0)
TORUS = {512: (8, 4, 8), 16: (2, 2, 2)}


def pick(k, values):
    out = jnp.int32(values[3])
    for i in (2, 1, 0):
        out = jnp.where(k == i, jnp.int32(values[i]), out)
    return out


def side_scalars(j, nb, rot, me, count, here):
    owner = nb // here
    off = lax.rem(owner - me + REACH + count, count)
    place = jnp.minimum(off, 2 * REACH) * here + (nb - owner * here)
    table = SIDE_TABLE[WANTED[j]]
    slot = pick(rot, [table[k][0] for k in range(4)])
    c1 = pick(rot, [table[k][1] & 1 for k in range(4)])
    c2 = pick(rot, [table[k][1] >> 1 for k in range(4)])
    return place * 4 + slot, c1, c2


def onehot(target, width):
    rows = target.shape[0]
    lanes = lax.broadcasted_iota(jnp.int32, (rows, width), 1)
    return jnp.where(lanes == target, 1.0, 0.0).astype(BF)


def rows_iota(rows):
    return lax.broadcasted_iota(jnp.int32, (rows, 1), 0)


def flip(c, x, last):
    return last * c + (1 - 2 * c) * x


def dot(a, b):
    return jnp.dot(a, b, preferred_element_type=F32)


def near_kernel(
    count, inp, cot, w, pool, center, zl, zr, wt, cpad, s_edge, r_edge
):
    me = lax.axis_index("patch")
    here = inp.shape[0]
    block = here * 4

    def near(o):
        return lax.rem(me + o + count, count)

    barrier = pltpu.get_barrier_semaphore()
    for o in NEAR:
        pl.semaphore_signal(barrier, inc=1, device_id=(near(o),), device_id_type=MESH)
    r64 = rows_iota(64)
    depth, along = r64 // 32, lax.rem(r64, 32)
    own = REACH * block

    def pack(p, carry):
        pool[own + p * 4] = inp[p, 0:2].reshape(64, 128)
        pool[own + p * 4 + 1] = inp[p, 30:32].reshape(64, 128)
        left = inp[p, :, 0:16, :].reshape(512, 128)
        pool[own + p * 4 + 2] = dot(onehot(along * 16 + depth, 512), left).astype(BF)
        right = inp[p, :, 16:32, :].reshape(512, 128)
        right = dot(onehot(along * 16 + depth + 14, 512), right)
        pool[own + p * 4 + 3] = right.astype(BF)
        return carry

    lax.fori_loop(0, here, pack, 0)
    pl.semaphore_wait(barrier, len(NEAR))
    edges = [
        pltpu.make_async_remote_copy(
            src_ref=pool.at[pl.ds(own, block)],
            dst_ref=pool.at[pl.ds((REACH - o) * block, block)],
            send_sem=s_edge.at[n],
            recv_sem=r_edge.at[n],
            device_id=(near(o),),
            device_id_type=MESH,
        )
        for n, o in enumerate(NEAR)
    ]
    for c in edges:
        c.start()

    for a in range(3):
        for b in range(3):
            piece = w[128 * (3 * a + b) : 128 * (3 * a + b) + 128]
            wt[128 * a : 128 * a + 128, 128 * b : 128 * b + 128] = piece.T
    cpad[0:4] = jnp.zeros((4, 32, 128), BF)
    cpad[36:40] = jnp.zeros((4, 32, 128), BF)
    cols = lax.broadcasted_iota(jnp.int32, (6, 32, 128), 1)

    def patch(p, carry):
        cpad[4:36] = cot[p]

        def chunk(n, c):
            y0 = n * 6
            lhs = jnp.concatenate(
                [cpad[pl.ds(y0 + 4 - 2 * a, 6)].reshape(192, 128) for a in range(3)],
                axis=1,
            )
            z = dot(lhs, wt[...])
            z0 = z[:, 0:128].reshape(6, 32, 128)
            z1 = z[:, 128:256].reshape(6, 32, 128)
            z2 = z[:, 256:384].reshape(6, 32, 128)
            zl[p, pl.ds(y0, 6)] = z0[:, 0:16].astype(BF)
            zr[p, pl.ds(y0, 6)] = z2[:, 16:32].astype(BF)
            total = z1 + jnp.where(cols < 30, pltpu.roll(z0, 30, 1), 0.0)
            total = total + jnp.where(cols >= 2, pltpu.roll(z2, 2, 1), 0.0)
            center[p, pl.ds(y0, 6)] = total
            return c

        lax.fori_loop(0, 6, chunk, 0)
        return carry

    lax.fori_loop(0, here, patch, 0)
    for c in edges:
        c.wait()


def far_kernel(
    sizes,
    factor,
    nb,
    rot,
    cor,
    inp,
    cot,
    w,
    bias,
    pool,
    center,
    zl,
    zr,
    out,
    ingrad,
    fin,
    arr,
    terms,
    tst,
    spots,
    xs,
    cpad,
    wacc,
    wloc,
    core_in,
    p_out,
    p_in,
    z_all,
    s_term,
    r_term,
    s_core,
    r_core,
    s_p,
    r_p,
    s_z,
    r_z,
    s_g,
    r_g,
    s_last,
    r_last,
):
    nz, nx, ny = sizes
    count = nz * nx * ny * 2
    plane = nx * ny
    me = lax.axis_index("patch")
    here = inp.shape[0]
    core = lax.rem(me, 2)
    y = lax.rem(me // 2, ny)
    x = lax.rem(me // (2 * ny), nx)
    z = me // (2 * ny * nx)
    q = x * ny + y
    mate = me + 1 - 2 * core
    block = here * 4
    mr, tr = 1024 // (2 * plane), 128 // (2 * plane)

    def peer_of(k):
        qk = lax.rem(x + k // ny, nx) * ny + lax.rem(y + lax.rem(k, ny), ny)
        return qk, me + 2 * (qk - q)

    def z_peer(k):
        return me + 2 * plane * (lax.rem(z + k, nz) - z)

    def near(o):
        return lax.rem(me + o + count, count)

    def copy(src, dst, send, recv, to):
        return pltpu.make_async_remote_copy(
            src_ref=src,
            dst_ref=dst,
            send_sem=send,
            recv_sem=recv,
            device_id=(to,),
            device_id_type=MESH,
        )

    barrier = pltpu.get_barrier_semaphore()

    def greet(peer):
        pl.semaphore_signal(barrier, inc=1, device_id=(peer,), device_id_type=MESH)

    def greet_plane(k, carry):
        greet(peer_of(k)[1])
        return carry

    for k in range(1, nz):
        greet(z_peer(k))
    lax.fori_loop(1, plane, greet_plane, 0)
    for o in NEAR:
        greet(near(o))
    greet(mate)

    cols = lax.broadcasted_iota(jnp.int32, (32, 32, 128), 1)

    def middle(p, total):
        here_in = inp[p]
        wide = here_in.astype(F32)
        xs[p, 2:34, :, 128:256] = here_in
        ahead = jnp.where(cols >= 2, pltpu.roll(wide, 2, 1), 0.0)
        xs[p, 2:34, :, 0:128] = ahead.astype(BF)
        behind = jnp.where(cols < 30, pltpu.roll(wide, 30, 1), 0.0)
        xs[p, 2:34, :, 256:384] = behind.astype(BF)
        cpad[p, 0:4] = jnp.zeros((4, 32, 128), BF)
        cpad[p, 36:40] = jnp.zeros((4, 32, 128), BF)
        here_cot = cot[p]
        cpad[p, 4:36] = here_cot
        return total + here_cot.astype(F32).reshape(128, 8, 128).sum(axis=0)

    bias8 = lax.fori_loop(0, here, middle, jnp.zeros((8, 128), F32))
    bias_here = jnp.sum(bias8, axis=0, keepdims=True)

    r192 = rows_iota(192)
    which, deep, on = r192 // 64, lax.rem(r192 // 32, 2), lax.rem(r192, 32)
    at = 2 * which + on
    r512 = rows_iota(512)
    line, place = r512 // 16, lax.rem(r512, 16)

    def halo(p, carry):
        def info(j):
            row, c1, c2 = side_scalars(j, nb[p, j], rot[p, j], me, count, here)
            return pool[row], c1, c2, cor[p, j] > 0

        for base, first in ((0, 0), (5, 34)):
            made = jnp.zeros((192, 128), F32)
            for j, c, inside in (
                (base, 30 + at, at < 2),
                (base + 1, at - 2, (at >= 2) & (at < 34)),
                (base + 2, at - 34, at >= 34),
            ):
                strip, c1, c2, present = info(j)
                target = 32 * flip(c1, deep, 1) + flip(c2, c, 31)
                target = jnp.where(inside & present, target, -1)
                made = made + dot(onehot(target, 64), strip)
            made = made.astype(BF)
            for b in range(3):
                piece = made[64 * b : 64 * b + 64].reshape(2, 32, 128)
                xs[p, first : first + 2, :, 128 * b : 128 * b + 128] = piece
        strip, c1, c2, present = info(3)
        target = 32 * flip(c1, place, 1) + flip(c2, line, 31)
        target = jnp.where((place < 2) & present, target, -1)
        made = dot(onehot(target, 64), strip).reshape(32, 16, 128)
        old = xs[p, 2:34, 0:16, 0:128].astype(F32)
        xs[p, 2:34, 0:16, 0:128] = (old + made).astype(BF)
        strip, c1, c2, present = info(4)
        target = 32 * flip(c1, place - 14, 1) + flip(c2, line, 31)
        target = jnp.where((place >= 14) & present, target, -1)
        made = dot(onehot(target, 64), strip).reshape(32, 16, 128)
        old = xs[p, 2:34, 16:32, 256:384].astype(F32)
        xs[p, 2:34, 16:32, 256:384] = (old + made).astype(BF)
        return carry

    lax.fori_loop(0, here, halo, 0)

    wacc[...] = jnp.zeros_like(wacc)

    def outer(n, carry):
        p, y0 = n // 3, lax.rem(n, 3) * 12
        lhs = xs[p, pl.ds(y0, 12)].reshape(384, 384)
        rhs = jnp.concatenate(
            [cpad[p, pl.ds(y0 + 4 - 2 * a, 12)].reshape(384, 128) for a in range(3)],
            axis=1,
        )
        wacc[...] += lax.dot_general(
            lhs, rhs, (((0,), (0,)), ((), ())), preferred_element_type=F32
        )
        return carry

    lax.fori_loop(0, here * 3, outer, 0)

    wide = wloc.shape[1] - mr
    row_t = lax.broadcasted_iota(jnp.int32, (wide, 128), 0)

    def split_bias(tail):
        b = tail[tr : tr + 1] + tail[tr + 1 : tr + 2]
        top = b.astype(BF).astype(F32)
        return jnp.where(row_t == tr, top, jnp.where(row_t == tr + 1, b - top, tail))

    def tap(t):
        a, b = t // 3, t % 3
        return wacc[128 * b : 128 * b + 128, 128 * a : 128 * a + 128]

    each = 128 // mr
    for t in range(8):
        wloc[t * each : (t + 1) * each, 0:mr] = tap(t).reshape(each, mr, 128)
    last = tap(8)
    for s in range(2 * plane):
        rows = [last[s * tr : (s + 1) * tr], bias_here]
        rows.append(jnp.zeros((wide - tr - 1, 128), F32))
        wloc[s, mr:] = jnp.concatenate(rows, axis=0)

    pl.semaphore_wait(barrier, nz - 1 + plane - 1 + len(NEAR) + 1)
    swap = copy(
        wloc.at[pl.ds((1 - core) * plane, plane)], core_in, s_core, r_core, mate
    )
    swap.start()

    def conv(n, carry):
        p, i0 = n // 4, lax.rem(n, 4) * 8
        lhs = jnp.concatenate(
            [xs[p, pl.ds(i0 + 2 * a, 8)].reshape(256, 384) for a in range(3)], axis=1
        )
        out[p, pl.ds(i0, 8)] = (dot(lhs, w[...]) + bias[...]).astype(BF).reshape(8, 32, 128)
        return carry

    lax.fori_loop(0, 2, conv, 0)
    swap.wait_recv()

    def pair(s, carry):
        slab = wloc[core * plane + s] + core_in[s]
        p_out[s, 0:mr] = slab[0:mr].astype(BF)
        p_out[s, mr:] = split_bias(slab[mr:]).astype(BF)
        return carry

    lax.fori_loop(0, plane, pair, 0)

    half = (nx // 2) * ny + ny // 2

    def order(n):
        return lax.rem(n // ny + nx // 2, nx) * ny + lax.rem(lax.rem(n, ny) + ny // 2, ny)

    def p_reduce(k):
        qk, peer = peer_of(k)
        return copy(p_out.at[qk], p_in.at[k - 1], s_p.at[k - 1], r_p.at[k - 1], peer)

    def every(fun, init):
        init = lax.fori_loop(0, half, lambda n, c: fun(order(n), c), init)
        return lax.fori_loop(half + 1, plane, lambda n, c: fun(order(n), c), init)

    def p_start(k, c):
        p_reduce(k).start()
        return c

    every(p_start, 0)

    r64 = rows_iota(64)
    depth, along = r64 // 32, lax.rem(r64, 32)

    def last_two(step, c):
        return jnp.where(c >= 30, step + c - 30, -1)

    def first_two(step, c):
        return jnp.where(c < 2, step + 14 + c, -1)

    def turn_back(p, carry):
        def back(j, target_of, piece):
            row, c1, c2 = side_scalars(j, nb[p, j], rot[p, j], me, count, here)
            target = target_of(flip(c1, depth, 1), flip(c2, along, 31))
            target = jnp.where(cor[p, j] > 0, target, -1)
            spots[p * 8 + j] = row
            tst[p * 8 + j] = dot(onehot(target, piece.shape[0]), piece)

        for base, lo in ((0, 0), (5, 34)):
            mid = center[p, lo : lo + 2].reshape(64, 128).astype(BF)
            ends = zl[p, lo : lo + 2].reshape(32, 128)
            back(base, lambda r, c: last_two(16 * r, c), ends)
            back(base + 1, lambda r, c: 32 * r + c, mid)
            ends = zr[p, lo : lo + 2].reshape(32, 128)
            back(base + 2, lambda r, c: first_two(16 * r, c), ends)
        back(3, lambda c, i: 16 * i + c, zl[p, 2:34].reshape(512, 128))
        back(4, lambda c, i: 16 * i + 14 + c, zr[p, 2:34].reshape(512, 128))
        return carry

    lax.fori_loop(0, here, turn_back, 0)

    def gather_terms(s, carry):
        total = jnp.zeros((64, 128), F32)
        for n in range(here * 8):
            total = total + jnp.where(spots[n] == s, 1.0, 0.0) * tst[n]
        terms[s] = total.astype(BF)
        return carry

    lax.fori_loop(0, 5 * block, gather_terms, 0)
    lax.fori_loop(2, 6, conv, 0)

    def p_add(k, c):
        p_reduce(k).wait_recv()
        return c + p_in[k - 1].astype(F32)

    z_all[z] = every(p_add, wloc[core * plane + q] + core_in[q])

    def z_gather(k):
        return copy(z_all.at[z], z_all.at[z], s_z.at[k - 1], r_z.at[k - 1], z_peer(k))

    for k in range(1, nz):
        z_gather(k).start()
    backs = [
        copy(
            terms.at[pl.ds((REACH + o) * block, block)],
            arr.at[n],
            s_term.at[n],
            r_term.at[n],
            near(o),
        )
        for n, o in enumerate(NEAR)
    ]
    for c in backs:
        c.start()
    lax.fori_loop(6, 4 * here, conv, 0)
    for k in range(1, nz):
        z_gather(k).wait_recv()
    slab = z_all[0]
    for n in range(1, nz):
        slab = slab + z_all[n]
    slab = slab * factor
    spot = core * plane + q
    fin[spot, 0:mr] = slab[0:mr].astype(BF)
    fin[spot, mr:] = split_bias(slab[mr:]).astype(BF)

    def p_gather(k):
        return copy(fin.at[spot], fin.at[spot], s_g.at[k - 1], r_g.at[k - 1], peer_of(k)[1])

    def g_start(k, c):
        p_gather(k).start()
        return c

    every(g_start, 0)
    for c in backs:
        c.wait_recv()

    def finish(p, carry):
        def pieces_of(slot):
            found = [terms[REACH * block + p * 4 + slot]]
            return found + [arr[n, p * 4 + slot] for n in range(len(NEAR))]

        def arrived(slot):
            total = jnp.zeros((64, 128), F32)
            for piece in pieces_of(slot):
                total = total + piece.astype(F32)
            return total.reshape(2, 32, 128)

        top, bottom = arrived(0), arrived(1)
        for slot, shift, lo in ((2, 0, 0), (3, 14, 16)):
            at_col = place - shift
            inside = (at_col >= 0) & (at_col < 2)
            spread = onehot(jnp.where(inside, 32 * at_col + line, -1), 64)
            made = jnp.zeros((512, 128), F32)
            for piece in pieces_of(slot):
                made = made + dot(spread, piece)
            total = center[p, 2:34, lo : lo + 16] + made.reshape(32, 16, 128)
            upper = total[0:2] + top[:, lo : lo + 16]
            lower = total[30:32] + bottom[:, lo : lo + 16]
            ingrad[p, 0:2, lo : lo + 16] = upper.astype(BF)
            ingrad[p, 2:30, lo : lo + 16] = total[2:30].astype(BF)
            ingrad[p, 30:32, lo : lo + 16] = lower.astype(BF)
        return carry

    lax.fori_loop(0, here, finish, 0)

    def g_wait(k, c):
        p_gather(k).wait_recv()
        return c

    every(g_wait, 0)
    mine = fin.at[pl.ds(core * plane, plane)]
    hand = copy(mine, mine, s_last, r_last, mate)
    hand.start()

    def sent(k, c):
        p_reduce(k).wait_send()
        p_gather(k).wait_send()
        return c

    every(sent, 0)
    for c in backs + [swap]:
        c.wait_send()
    for k in range(1, nz):
        z_gather(k).wait_send()
    hand.wait()


def body(count, inputs, cotangent, weights, bias_vector, neighbours, rotations, corners):
    here, length, _, chans = inputs.shape
    sizes = TORUS[count]
    nz, nx, ny = sizes
    plane = nx * ny
    factor = 1.0 / (length * math.sqrt(here * count))
    block = here * 4
    smem = pl.BlockSpec(memory_space=pltpu.SMEM)
    vmem = pl.BlockSpec(memory_space=pltpu.VMEM)
    dma = pltpu.SemaphoreType.DMA
    flat = weights.reshape(9 * chans, chans)
    pool, center, zl, zr = pl.pallas_call(
        functools.partial(near_kernel, count),
        out_shape=(
            jax.ShapeDtypeStruct((5 * block, 64, chans), BF),
            jax.ShapeDtypeStruct((here, 36, 32, chans), F32),
            jax.ShapeDtypeStruct((here, 36, 16, chans), BF),
            jax.ShapeDtypeStruct((here, 36, 16, chans), BF),
        ),
        in_specs=[vmem] * 3,
        out_specs=(vmem,) * 4,
        scratch_shapes=[
            pltpu.VMEM((3 * chans, 3 * chans), BF),
            pltpu.VMEM((40, 32, chans), BF),
            dma((len(NEAR),)),
            dma((len(NEAR),)),
        ],
        compiler_params=pltpu.CompilerParams(
            collective_id=1, has_side_effects=True, vmem_limit_bytes=16 * 2**20
        ),
    )(inputs, cotangent, flat)

    mr, tr = 1024 // (2 * plane), 128 // (2 * plane)
    rows = mr + -(-(tr + 2) // 8) * 8
    outputs, input_grad, fin = pl.pallas_call(
        functools.partial(far_kernel, sizes, factor),
        out_shape=(
            jax.ShapeDtypeStruct(inputs.shape, BF),
            jax.ShapeDtypeStruct(inputs.shape, BF),
            jax.ShapeDtypeStruct((2 * plane, rows, chans), BF),
        ),
        in_specs=[smem] * 3 + [vmem] * 8,
        out_specs=(vmem,) * 3,
        scratch_shapes=[
            pltpu.VMEM((len(NEAR), block, 64, chans), BF),
            pltpu.VMEM((5 * block, 64, chans), BF),
            pltpu.VMEM((here * 8, 64, chans), F32),
            pltpu.SMEM((here * 8,), jnp.int32),
            pltpu.VMEM((here, 36, 32, 3 * chans), BF),
            pltpu.VMEM((here, 40, 32, chans), BF),
            pltpu.VMEM((3 * chans, 3 * chans), F32),
            pltpu.VMEM((2 * plane, rows, chans), F32),
            pltpu.VMEM((plane, rows, chans), F32),
            pltpu.VMEM((plane, rows, chans), BF),
            pltpu.VMEM((plane - 1, rows, chans), BF),
            pltpu.VMEM((nz, rows, chans), F32),
            dma((len(NEAR),)),
            dma((len(NEAR),)),
            dma,
            dma,
            dma((plane - 1,)),
            dma((plane - 1,)),
            dma((nz - 1,)),
            dma((nz - 1,)),
            dma((plane - 1,)),
            dma((plane - 1,)),
            dma,
            dma,
        ],
        compiler_params=pltpu.CompilerParams(
            collective_id=0, has_side_effects=True, vmem_limit_bytes=26 * 2**20
        ),
    )(
        neighbours,
        rotations,
        corners,
        inputs,
        cotangent,
        flat,
        bias_vector.reshape(1, chans),
        pool,
        center,
        zl,
        zr,
    )
    main = fin[:, 0:mr].reshape(8 * chans, chans)
    rest = fin[:, mr : mr + tr].reshape(chans, chans)
    weight_grad = jnp.concatenate([main, rest], axis=0).astype(F32)
    bias_grad = fin[0, mr + tr].astype(F32) + fin[0, mr + tr + 1].astype(F32)
    return (outputs, input_grad, weight_grad.reshape(weights.shape), bias_grad)


def solution(mesh):
    in_specs = (
        P("patch", None, None, None),
        P("patch", None, None, None),
        P(),
        P(),
        P("patch", None),
        P("patch", None),
        P("patch", None),
    )
    out_specs = (P("patch", None, None, None), P("patch", None, None, None), P(), P())
    return jax.shard_map(
        functools.partial(body, mesh.shape["patch"]),
        mesh=mesh,
        in_specs=in_specs,
        out_specs=out_specs,
        check_vma=False,
    )
```

```python
import functools
import math

import jax
import jax.numpy as jnp
from jax import lax
from jax.experimental import pallas as pl
from jax.experimental.pallas import tpu as pltpu
from jax.sharding import PartitionSpec as P

REACH = 2
NEAR = (-2, -1, 1, 2)
MESH = pl.DeviceIdType.MESH
BF = jnp.bfloat16
F32 = jnp.float32
SIDE_TABLE = (
    ((0, 0), (3, 1), (1, 3), (2, 2)),
    ((1, 0), (2, 1), (0, 3), (3, 2)),
    ((2, 0), (0, 2), (3, 3), (1, 1)),
    ((3, 0), (1, 2), (2, 3), (0, 1)),
)
WANTED = (1, 1, 1, 3, 2, 0, 0, 0)
TORUS = {512: (8, 4, 8), 16: (2, 2, 2)}


def pick(k, values):
    out = jnp.int32(values[3])
    for i in (2, 1, 0):
        out = jnp.where(k == i, jnp.int32(values[i]), out)
    return out


def side_scalars(j, nb, rot, me, count, here):
    owner = nb // here
    off = lax.rem(owner - me + REACH + count, count)
    place = jnp.minimum(off, 2 * REACH) * here + (nb - owner * here)
    table = SIDE_TABLE[WANTED[j]]
    slot = pick(rot, [table[k][0] for k in range(4)])
    c1 = pick(rot, [table[k][1] & 1 for k in range(4)])
    c2 = pick(rot, [table[k][1] >> 1 for k in range(4)])
    return place * 4 + slot, c1, c2


def onehot(target, width):
    rows = target.shape[0]
    lanes = lax.broadcasted_iota(jnp.int32, (rows, width), 1)
    return jnp.where(lanes == target, 1.0, 0.0).astype(BF)


def rows_iota(rows):
    return lax.broadcasted_iota(jnp.int32, (rows, 1), 0)


def flip(c, x, last):
    return last * c + (1 - 2 * c) * x


def dot(a, b):
    return jnp.dot(a, b, preferred_element_type=F32)


def main_kernel(
    sizes,
    factor,
    nb_in,
    rot_in,
    cor_in,
    inp_in,
    cot_in,
    w_in,
    bias_in,
    out_o,
    ingrad_o,
    fin_o,
    out,
    ingrad,
    fin,
    nb,
    rot,
    cor,
    inp,
    w,
    bias,
    wt,
    pool,
    center,
    zl,
    zr,
    arr,
    terms,
    tst,
    spots,
    xs,
    cpad,
    wacc,
    wloc,
    core_in,
    p_out,
    p_in,
    z_all,
    s_load,
    s_store,
    s_edge,
    r_edge,
    s_term,
    r_term,
    s_core,
    r_core,
    s_p,
    r_p,
    s_z,
    r_z,
    s_g,
    r_g,
    s_last,
    r_last,
):
    nz, nx, ny = sizes
    count = nz * nx * ny * 2
    plane = nx * ny
    me = lax.axis_index("patch")
    here = inp.shape[0]
    loads = [
        pltpu.make_async_copy(src, dst, s_load.at[n])
        for n, (src, dst) in enumerate(
            [(inp_in, inp), (nb_in, nb), (rot_in, rot), (cor_in, cor)]
            + [(w_in, w), (bias_in, bias)]
            + [(cot_in.at[p], cpad.at[p, 4:36]) for p in range(here)]
        )
    ]
    for c in loads:
        c.start()
    core = lax.rem(me, 2)
    y = lax.rem(me // 2, ny)
    x = lax.rem(me // (2 * ny), nx)
    z = me // (2 * ny * nx)
    q = x * ny + y
    mate = me + 1 - 2 * core
    block = here * 4
    mr, tr = 1024 // (2 * plane), 128 // (2 * plane)

    def peer_of(k):
        qk = lax.rem(x + k // ny, nx) * ny + lax.rem(y + lax.rem(k, ny), ny)
        return qk, me + 2 * (qk - q)

    def z_peer(k):
        return me + 2 * plane * (lax.rem(z + k, nz) - z)

    def near(o):
        return lax.rem(me + o + count, count)

    def copy(src, dst, send, recv, to):
        return pltpu.make_async_remote_copy(
            src_ref=src,
            dst_ref=dst,
            send_sem=send,
            recv_sem=recv,
            device_id=(to,),
            device_id_type=MESH,
        )

    barrier = pltpu.get_barrier_semaphore()

    def greet(peer):
        pl.semaphore_signal(barrier, inc=1, device_id=(peer,), device_id_type=MESH)

    def greet_plane(k, carry):
        greet(peer_of(k)[1])
        return carry

    for k in range(1, nz):
        greet(z_peer(k))
    lax.fori_loop(1, plane, greet_plane, 0)
    for o in NEAR:
        greet(near(o))
    greet(mate)

    r64 = rows_iota(64)
    depth, along = r64 // 32, lax.rem(r64, 32)
    own = REACH * block
    loads[0].wait()

    def pack(p, carry):
        pool[own + p * 4] = inp[p, 0:2].reshape(64, 128)
        pool[own + p * 4 + 1] = inp[p, 30:32].reshape(64, 128)
        left = inp[p, :, 0:16, :].reshape(512, 128)
        pool[own + p * 4 + 2] = dot(onehot(along * 16 + depth, 512), left).astype(BF)
        right = inp[p, :, 16:32, :].reshape(512, 128)
        right = dot(onehot(along * 16 + depth + 14, 512), right)
        pool[own + p * 4 + 3] = right.astype(BF)
        return carry

    lax.fori_loop(0, here, pack, 0)
    pl.semaphore_wait(barrier, nz - 1 + plane - 1 + len(NEAR) + 1)
    edges = [
        copy(
            pool.at[pl.ds(own, block)],
            pool.at[pl.ds((REACH - o) * block, block)],
            s_edge.at[n],
            r_edge.at[n],
            near(o),
        )
        for n, o in enumerate(NEAR)
    ]
    for c in edges:
        c.start()
    for c in loads[1:]:
        c.wait()

    cols = lax.broadcasted_iota(jnp.int32, (32, 32, 128), 1)

    def middle(p, total):
        here_in = inp[p]
        wide = here_in.astype(F32)
        xs[p, 2:34, :, 128:256] = here_in
        ahead = jnp.where(cols >= 2, pltpu.roll(wide, 2, 1), 0.0)
        xs[p, 2:34, :, 0:128] = ahead.astype(BF)
        behind = jnp.where(cols < 30, pltpu.roll(wide, 30, 1), 0.0)
        xs[p, 2:34, :, 256:384] = behind.astype(BF)
        cpad[p, 0:4] = jnp.zeros((4, 32, 128), BF)
        cpad[p, 36:40] = jnp.zeros((4, 32, 128), BF)
        here_cot = cpad[p, 4:36]
        return total + here_cot.astype(F32).reshape(128, 8, 128).sum(axis=0)

    bias8 = lax.fori_loop(0, here, middle, jnp.zeros((8, 128), F32))
    bias_here = jnp.sum(bias8, axis=0, keepdims=True)
    wacc[...] = jnp.zeros_like(wacc)

    def outer_dot(a, b):
        return lax.dot_general(
            a, b, (((0,), (0,)), ((), ())), preferred_element_type=F32
        )

    def inner(n, carry):
        p, y0 = n // 4, lax.rem(n, 4) * 8 + 2
        lhs = xs[p, pl.ds(y0, 8)].reshape(256, 384)
        rhs = jnp.concatenate(
            [cpad[p, pl.ds(y0 + 4 - 2 * a, 8)].reshape(256, 128) for a in range(3)],
            axis=1,
        )
        wacc[...] += outer_dot(lhs, rhs)
        return carry

    lax.fori_loop(0, here * 4, inner, 0)

    for a in range(3):
        for b in range(3):
            piece = w[128 * (3 * a + b) : 128 * (3 * a + b) + 128]
            wt[128 * a : 128 * a + 128, 128 * b : 128 * b + 128] = piece.T
    cols6 = lax.broadcasted_iota(jnp.int32, (6, 32, 128), 1)

    def spread_back(n, carry):
        p, y0 = n // 6, lax.rem(n, 6) * 6
        lhs = jnp.concatenate(
            [cpad[p, pl.ds(y0 + 4 - 2 * a, 6)].reshape(192, 128) for a in range(3)],
            axis=1,
        )
        got = dot(lhs, wt[...])
        z0 = got[:, 0:128].reshape(6, 32, 128)
        z1 = got[:, 128:256].reshape(6, 32, 128)
        z2 = got[:, 256:384].reshape(6, 32, 128)
        zl[p, pl.ds(y0, 6)] = z0[:, 0:16].astype(BF)
        zr[p, pl.ds(y0, 6)] = z2[:, 16:32].astype(BF)
        total = z1 + jnp.where(cols6 < 30, pltpu.roll(z0, 30, 1), 0.0)
        total = total + jnp.where(cols6 >= 2, pltpu.roll(z2, 2, 1), 0.0)
        center[p, pl.ds(y0, 6)] = total
        return carry

    lax.fori_loop(0, here * 3, spread_back, 0)
    for c in edges:
        c.wait_recv()

    r192 = rows_iota(192)
    which, deep, on = r192 // 64, lax.rem(r192 // 32, 2), lax.rem(r192, 32)
    at = 2 * which + on
    r512 = rows_iota(512)
    line, place = r512 // 16, lax.rem(r512, 16)

    def halo(p, carry):
        def info(j):
            row, c1, c2 = side_scalars(j, nb[p, j], rot[p, j], me, count, here)
            return pool[row], c1, c2, cor[p, j] > 0

        for base, first in ((0, 0), (5, 34)):
            made = jnp.zeros((192, 128), F32)
            for j, c, inside in (
                (base, 30 + at, at < 2),
                (base + 1, at - 2, (at >= 2) & (at < 34)),
                (base + 2, at - 34, at >= 34),
            ):
                strip, c1, c2, present = info(j)
                target = 32 * flip(c1, deep, 1) + flip(c2, c, 31)
                target = jnp.where(inside & present, target, -1)
                made = made + dot(onehot(target, 64), strip)
            made = made.astype(BF)
            for b in range(3):
                piece = made[64 * b : 64 * b + 64].reshape(2, 32, 128)
                xs[p, first : first + 2, :, 128 * b : 128 * b + 128] = piece
        wacc[:, 0:128] += outer_dot(
            xs[p, 0:2].reshape(64, 384), cpad[p, 4:6].reshape(64, 128)
        )
        wacc[:, 256:384] += outer_dot(
            xs[p, 34:36].reshape(64, 384), cpad[p, 34:36].reshape(64, 128)
        )
        for j, shift, lo, lane in ((3, 0, 0, 0), (4, 14, 16, 256)):
            strip, c1, c2, present = info(j)
            side = place - shift
            target = 32 * flip(c1, side, 1) + flip(c2, line, 31)
            inside = (side >= 0) & (side < 2) & present
            made = dot(onehot(jnp.where(inside, target, -1), 64), strip)
            rhs = jnp.concatenate(
                [
                    cpad[p, 6 - 2 * a : 38 - 2 * a, lo : lo + 16].reshape(512, 128)
                    for a in range(3)
                ],
                axis=1,
            )
            wacc[lane : lane + 128] += outer_dot(made.astype(BF), rhs)
            old = xs[p, 2:34, lo : lo + 16, lane : lane + 128].astype(F32)
            xs[p, 2:34, lo : lo + 16, lane : lane + 128] = (
                old + made.reshape(32, 16, 128)
            ).astype(BF)
        return carry

    lax.fori_loop(0, here, halo, 0)

    wide = wloc.shape[1] - mr
    row_t = lax.broadcasted_iota(jnp.int32, (wide, 128), 0)

    def split_bias(tail):
        b = tail[tr : tr + 1] + tail[tr + 1 : tr + 2]
        top = b.astype(BF).astype(F32)
        return jnp.where(row_t == tr, top, jnp.where(row_t == tr + 1, b - top, tail))

    def tap(t):
        a, b = t // 3, t % 3
        return wacc[128 * b : 128 * b + 128, 128 * a : 128 * a + 128]

    each = 128 // mr
    for t in range(8):
        wloc[t * each : (t + 1) * each, 0:mr] = tap(t).reshape(each, mr, 128)
    last = tap(8)
    for s in range(2 * plane):
        rows = [last[s * tr : (s + 1) * tr], bias_here]
        rows.append(jnp.zeros((wide - tr - 1, 128), F32))
        wloc[s, mr:] = jnp.concatenate(rows, axis=0)

    swap = copy(
        wloc.at[pl.ds((1 - core) * plane, plane)], core_in, s_core, r_core, mate
    )
    swap.start()

    def conv(n, carry):
        p, i0 = n // 4, lax.rem(n, 4) * 8
        lhs = jnp.concatenate(
            [xs[p, pl.ds(i0 + 2 * a, 8)].reshape(256, 384) for a in range(3)], axis=1
        )
        out[p, pl.ds(i0, 8)] = (dot(lhs, w[...]) + bias[...]).astype(BF).reshape(8, 32, 128)
        return carry

    lax.fori_loop(here * 3, here * 4, spread_back, 0)
    swap.wait_recv()

    half = (nx // 2) * ny + ny // 2

    def order(n):
        return lax.rem(n // ny + nx // 2, nx) * ny + lax.rem(lax.rem(n, ny) + ny // 2, ny)

    def p_reduce(k):
        qk, peer = peer_of(k)
        return copy(p_out.at[qk], p_in.at[k - 1], s_p.at[k - 1], r_p.at[k - 1], peer)

    def every(fun, init):
        init = lax.fori_loop(0, half, lambda n, c: fun(order(n), c), init)
        return lax.fori_loop(half + 1, plane, lambda n, c: fun(order(n), c), init)

    def p_start(k, c):
        qk = peer_of(k)[0]
        slab = wloc[core * plane + qk] + core_in[qk]
        p_out[qk, 0:mr] = slab[0:mr].astype(BF)
        p_out[qk, mr:] = split_bias(slab[mr:]).astype(BF)
        p_reduce(k).start()
        return c

    every(p_start, 0)
    lax.fori_loop(here * 4, here * 6, spread_back, 0)

    def last_two(step, c):
        return jnp.where(c >= 30, step + c - 30, -1)

    def first_two(step, c):
        return jnp.where(c < 2, step + 14 + c, -1)

    def turn_back(p, carry):
        def back(j, target_of, piece):
            row, c1, c2 = side_scalars(j, nb[p, j], rot[p, j], me, count, here)
            target = target_of(flip(c1, depth, 1), flip(c2, along, 31))
            target = jnp.where(cor[p, j] > 0, target, -1)
            spots[p * 8 + j] = row
            tst[p * 8 + j] = dot(onehot(target, piece.shape[0]), piece)

        for base, lo in ((0, 0), (5, 34)):
            mid = center[p, lo : lo + 2].reshape(64, 128).astype(BF)
            ends = zl[p, lo : lo + 2].reshape(32, 128)
            back(base, lambda r, c: last_two(16 * r, c), ends)
            back(base + 1, lambda r, c: 32 * r + c, mid)
            ends = zr[p, lo : lo + 2].reshape(32, 128)
            back(base + 2, lambda r, c: first_two(16 * r, c), ends)
        back(3, lambda c, i: 16 * i + c, zl[p, 2:34].reshape(512, 128))
        back(4, lambda c, i: 16 * i + 14 + c, zr[p, 2:34].reshape(512, 128))
        return carry

    def gather_terms(s, carry):
        total = jnp.zeros((64, 128), F32)
        for n in range(here * 8):
            total = total + jnp.where(spots[n] == s, 1.0, 0.0) * tst[n]
        terms[s] = total.astype(BF)
        return carry

    lax.fori_loop(0, here, turn_back, 0)
    lax.fori_loop(0, 5 * block, gather_terms, 0)

    def p_add(k, c):
        p_reduce(k).wait_recv()
        return c + p_in[k - 1].astype(F32)

    z_all[z] = every(p_add, wloc[core * plane + q] + core_in[q])

    def z_gather(k):
        return copy(z_all.at[z], z_all.at[z], s_z.at[k - 1], r_z.at[k - 1], z_peer(k))

    for k in range(1, nz):
        z_gather(k).start()
    backs = [
        copy(
            terms.at[pl.ds((REACH + o) * block, block)],
            arr.at[n],
            s_term.at[n],
            r_term.at[n],
            near(o),
        )
        for n, o in enumerate(NEAR)
    ]
    for c in backs:
        c.start()

    lax.fori_loop(0, 4 * here, conv, 0)
    stores = [pltpu.make_async_copy(out, out_o, s_store.at[0])]
    stores[0].start()
    for k in range(1, nz):
        z_gather(k).wait_recv()
    slab = z_all[0]
    for n in range(1, nz):
        slab = slab + z_all[n]
    slab = slab * factor
    spot = core * plane + q
    fin[spot, 0:mr] = slab[0:mr].astype(BF)
    fin[spot, mr:] = split_bias(slab[mr:]).astype(BF)

    def p_gather(k):
        return copy(fin.at[spot], fin.at[spot], s_g.at[k - 1], r_g.at[k - 1], peer_of(k)[1])

    def g_start(k, c):
        p_gather(k).start()
        return c

    every(g_start, 0)
    for c in backs:
        c.wait_recv()

    def finish(p, carry):
        def pieces_of(slot):
            found = [terms[REACH * block + p * 4 + slot]]
            return found + [arr[n, p * 4 + slot] for n in range(len(NEAR))]

        def arrived(slot):
            total = jnp.zeros((64, 128), F32)
            for piece in pieces_of(slot):
                total = total + piece.astype(F32)
            return total.reshape(2, 32, 128)

        top, bottom = arrived(0), arrived(1)
        for slot, shift, lo in ((2, 0, 0), (3, 14, 16)):
            at_col = place - shift
            inside = (at_col >= 0) & (at_col < 2)
            spread = onehot(jnp.where(inside, 32 * at_col + line, -1), 64)
            made = jnp.zeros((512, 128), F32)
            for piece in pieces_of(slot):
                made = made + dot(spread, piece)
            total = center[p, 2:34, lo : lo + 16] + made.reshape(32, 16, 128)
            upper = total[0:2] + top[:, lo : lo + 16]
            lower = total[30:32] + bottom[:, lo : lo + 16]
            ingrad[p, 0:2, lo : lo + 16] = upper.astype(BF)
            ingrad[p, 2:30, lo : lo + 16] = total[2:30].astype(BF)
            ingrad[p, 30:32, lo : lo + 16] = lower.astype(BF)
        return carry

    lax.fori_loop(0, here, finish, 0)
    stores.append(pltpu.make_async_copy(ingrad, ingrad_o, s_store.at[1]))
    stores[1].start()

    def g_wait(k, c):
        p_gather(k).wait_recv()
        return c

    every(g_wait, 0)
    mine = pl.ds(core * plane, plane)
    hand = copy(fin.at[mine], fin_o.at[mine], s_last, r_last, mate)
    hand.start()
    stores.append(pltpu.make_async_copy(fin.at[mine], fin_o.at[mine], s_store.at[2]))
    stores[2].start()

    def sent(k, c):
        p_reduce(k).wait_send()
        p_gather(k).wait_send()
        return c

    every(sent, 0)
    for c in edges + backs + [swap]:
        c.wait_send()
    for k in range(1, nz):
        z_gather(k).wait_send()
    for c in stores:
        c.wait()
    hand.wait()


def write_kernel(
    mr, tr, out, ingrad, fin_o, out_o, ingrad_o, wgrad_o, bgrad, fin, wide, sems
):
    here = out.shape[0]
    load = pltpu.make_async_copy(fin_o, fin, sems.at[0])
    load.start()
    moves = []
    for p in range(here):
        for n, (src, dst) in enumerate(((out, out_o), (ingrad, ingrad_o))):
            moves.append(
                pltpu.make_async_copy(src.at[p], dst.at[p], sems.at[2 + 2 * p + n])
            )
            moves[-1].start()
    load.wait()
    slabs = fin.shape[0]
    wide[0:1024] = fin[:, 0:mr].astype(F32).reshape(1024, 128)
    for s in range(slabs):
        tail = fin[s, mr:].astype(F32)
        wide[1024 + tr * s : 1024 + tr * (s + 1)] = tail[0:tr]
    moves.append(pltpu.make_async_copy(wide, wgrad_o, sems.at[1]))
    moves[-1].start()
    tail = fin[0, mr:].astype(F32)
    bgrad[...] = tail[tr : tr + 1] + tail[tr + 1 : tr + 2]
    for c in moves:
        c.wait()


def body(count, inputs, cotangent, weights, bias_vector, neighbours, rotations, corners):
    here, length, _, chans = inputs.shape
    sizes = TORUS[count]
    nz, nx, ny = sizes
    plane = nx * ny
    factor = 1.0 / (length * math.sqrt(here * count))
    block = here * 4
    hbm = pl.BlockSpec(memory_space=pltpu.HBM)
    vmem = pl.BlockSpec(memory_space=pltpu.VMEM)
    dma = pltpu.SemaphoreType.DMA
    mr, tr = 1024 // (2 * plane), 128 // (2 * plane)
    rows = mr + -(-(tr + 2) // 8) * 8
    near = len(NEAR)
    wires = [near, near, None, plane - 1, nz - 1, plane - 1, None]
    outputs, input_grad, fin = pl.pallas_call(
        functools.partial(main_kernel, sizes, factor),
        out_shape=(
            jax.ShapeDtypeStruct(inputs.shape, BF),
            jax.ShapeDtypeStruct(inputs.shape, BF),
            jax.ShapeDtypeStruct((2 * plane, rows, chans), BF),
        ),
        in_specs=[hbm] * 7,
        out_specs=(hbm,) * 3,
        scratch_shapes=[
            pltpu.VMEM(inputs.shape, BF),
            pltpu.VMEM(inputs.shape, BF),
            pltpu.VMEM((2 * plane, rows, chans), BF),
            pltpu.SMEM((here, 8), jnp.int32),
            pltpu.SMEM((here, 8), jnp.int32),
            pltpu.SMEM((here, 8), jnp.int32),
            pltpu.VMEM(inputs.shape, BF),
            pltpu.VMEM((9 * chans, chans), BF),
            pltpu.VMEM((1, chans), F32),
            pltpu.VMEM((3 * chans, 3 * chans), BF),
            pltpu.VMEM((5 * block, 64, chans), BF),
            pltpu.VMEM((here, 36, 32, chans), F32),
            pltpu.VMEM((here, 36, 16, chans), BF),
            pltpu.VMEM((here, 36, 16, chans), BF),
            pltpu.VMEM((near, block, 64, chans), BF),
            pltpu.VMEM((5 * block, 64, chans), BF),
            pltpu.VMEM((here * 8, 64, chans), F32),
            pltpu.SMEM((here * 8,), jnp.int32),
            pltpu.VMEM((here, 36, 32, 3 * chans), BF),
            pltpu.VMEM((here, 40, 32, chans), BF),
            pltpu.VMEM((3 * chans, 3 * chans), F32),
            pltpu.VMEM((2 * plane, rows, chans), F32),
            pltpu.VMEM((plane, rows, chans), F32),
            pltpu.VMEM((plane, rows, chans), BF),
            pltpu.VMEM((plane - 1, rows, chans), BF),
            pltpu.VMEM((nz, rows, chans), F32),
            dma((6 + here,)),
            dma((3,)),
        ]
        + [dma if n is None else dma((n,)) for n in wires for _ in range(2)],
        compiler_params=pltpu.CompilerParams(
            collective_id=0, has_side_effects=True, vmem_limit_bytes=56 * 2**20
        ),
    )(
        neighbours,
        rotations,
        corners,
        inputs,
        cotangent,
        weights.reshape(9 * chans, chans),
        bias_vector.reshape(1, chans),
    )
    outputs, input_grad, weight_grad, bias_grad = pl.pallas_call(
        functools.partial(write_kernel, mr, tr),
        out_shape=(
            jax.ShapeDtypeStruct(inputs.shape, BF),
            jax.ShapeDtypeStruct(inputs.shape, BF),
            jax.ShapeDtypeStruct((9 * chans, chans), F32),
            jax.ShapeDtypeStruct((1, chans), F32),
        ),
        in_specs=[hbm] * 3,
        out_specs=(hbm, hbm, hbm, vmem),
        scratch_shapes=[
            pltpu.VMEM((2 * plane, rows, chans), BF),
            pltpu.VMEM((9 * chans, chans), F32),
            dma((2 + 2 * here,)),
        ],
        compiler_params=pltpu.CompilerParams(vmem_limit_bytes=56 * 2**20),
    )(outputs, input_grad, fin)
    return (
        outputs,
        input_grad,
        weight_grad.reshape(weights.shape),
        bias_grad.reshape(bias_vector.shape),
    )


def solution(mesh):
    in_specs = (
        P("patch", None, None, None),
        P("patch", None, None, None),
        P(),
        P(),
        P("patch", None),
        P("patch", None),
        P("patch", None),
    )
    out_specs = (P("patch", None, None, None), P("patch", None, None, None), P(), P())
    return jax.shard_map(
        functools.partial(body, mesh.shape["patch"]),
        mesh=mesh,
        in_specs=in_specs,
        out_specs=out_specs,
        check_vma=False,
    )
```

```python
import functools
import math

import jax
import jax.numpy as jnp
from jax import lax
from jax.experimental import pallas as pl
from jax.experimental.pallas import tpu as pltpu
from jax.sharding import PartitionSpec as P

REACH = 2
NEAR = (-2, -1, 1, 2)
MESH = pl.DeviceIdType.MESH
BF = jnp.bfloat16
F32 = jnp.float32
SIDE_TABLE = (
    ((0, 0), (3, 1), (1, 3), (2, 2)),
    ((1, 0), (2, 1), (0, 3), (3, 2)),
    ((2, 0), (0, 2), (3, 3), (1, 1)),
    ((3, 0), (1, 2), (2, 3), (0, 1)),
)
WANTED = (1, 1, 1, 3, 2, 0, 0, 0)
TORUS = {512: (8, 4, 8), 16: (2, 2, 2)}


def pick(k, values):
    out = jnp.int32(values[3])
    for i in (2, 1, 0):
        out = jnp.where(k == i, jnp.int32(values[i]), out)
    return out


def side_scalars(j, nb, rot, me, count, here):
    owner = nb // here
    off = lax.rem(owner - me + REACH + count, count)
    place = jnp.minimum(off, 2 * REACH) * here + (nb - owner * here)
    table = SIDE_TABLE[WANTED[j]]
    slot = pick(rot, [table[k][0] for k in range(4)])
    c1 = pick(rot, [table[k][1] & 1 for k in range(4)])
    c2 = pick(rot, [table[k][1] >> 1 for k in range(4)])
    return place * 4 + slot, c1, c2


def onehot(target, width):
    rows = target.shape[0]
    lanes = lax.broadcasted_iota(jnp.int32, (rows, width), 1)
    return jnp.where(lanes == target, 1.0, 0.0).astype(BF)


def rows_iota(rows):
    return lax.broadcasted_iota(jnp.int32, (rows, 1), 0)


def flip(c, x, last):
    return last * c + (1 - 2 * c) * x


def dot(a, b):
    return jnp.dot(a, b, preferred_element_type=F32)


def main_kernel(
    sizes,
    factor,
    nb_in,
    rot_in,
    cor_in,
    inp_in,
    cot_in,
    w_in,
    bias_in,
    out_o,
    ingrad_o,
    fin_o,
    out,
    ingrad,
    fin,
    nb,
    rot,
    cor,
    inp,
    w,
    bias,
    wt,
    pool,
    center,
    zl,
    zr,
    arr,
    terms,
    tst,
    spots,
    xs,
    cpad,
    wacc,
    wloc,
    core_in,
    p_out,
    p_in,
    z_all,
    s_load,
    s_store,
    s_edge,
    r_edge,
    s_term,
    r_term,
    s_core,
    r_core,
    s_p,
    r_p,
    s_z,
    r_z,
    s_g,
    r_g,
    s_last,
    r_last,
):
    nz, nx, ny = sizes
    count = nz * nx * ny * 2
    plane = nx * ny
    me = lax.axis_index("patch")
    here = inp.shape[0]
    loads = [
        pltpu.make_async_copy(src, dst, s_load.at[n])
        for n, (src, dst) in enumerate(
            [(inp_in, inp), (nb_in, nb), (rot_in, rot), (cor_in, cor)]
            + [(w_in, w), (bias_in, bias)]
            + [(cot_in.at[p], cpad.at[p, 4:36]) for p in range(here)]
        )
    ]
    for c in loads:
        c.start()
    core = lax.rem(me, 2)
    y = lax.rem(me // 2, ny)
    x = lax.rem(me // (2 * ny), nx)
    z = me // (2 * ny * nx)
    q = x * ny + y
    mate = me + 1 - 2 * core
    block = here * 4
    mr, tr = 1024 // (2 * plane), 128 // (2 * plane)

    def peer_of(k):
        qk = lax.rem(x + k // ny, nx) * ny + lax.rem(y + lax.rem(k, ny), ny)
        return qk, me + 2 * (qk - q)

    def z_peer(k):
        return me + 2 * plane * (lax.rem(z + k, nz) - z)

    def near(o):
        return lax.rem(me + o + count, count)

    def copy(src, dst, send, recv, to):
        return pltpu.make_async_remote_copy(
            src_ref=src,
            dst_ref=dst,
            send_sem=send,
            recv_sem=recv,
            device_id=(to,),
            device_id_type=MESH,
        )

    barrier = pltpu.get_barrier_semaphore()

    def greet(peer):
        pl.semaphore_signal(barrier, inc=1, device_id=(peer,), device_id_type=MESH)

    def greet_plane(k, carry):
        greet(peer_of(k)[1])
        return carry

    for k in range(1, nz):
        greet(z_peer(k))
    lax.fori_loop(1, plane, greet_plane, 0)
    for o in NEAR:
        greet(near(o))
    greet(mate)

    r64 = rows_iota(64)
    depth, along = r64 // 32, lax.rem(r64, 32)
    own = REACH * block
    loads[0].wait()

    def pack(p, carry):
        pool[own + p * 4] = inp[p, 0:2].reshape(64, 128)
        pool[own + p * 4 + 1] = inp[p, 30:32].reshape(64, 128)
        left = inp[p, :, 0:16, :].reshape(512, 128)
        pool[own + p * 4 + 2] = dot(onehot(along * 16 + depth, 512), left).astype(BF)
        right = inp[p, :, 16:32, :].reshape(512, 128)
        right = dot(onehot(along * 16 + depth + 14, 512), right)
        pool[own + p * 4 + 3] = right.astype(BF)
        return carry

    lax.fori_loop(0, here, pack, 0)
    pl.semaphore_wait(barrier, nz - 1 + plane - 1 + len(NEAR) + 1)
    edges = [
        copy(
            pool.at[pl.ds(own, block)],
            pool.at[pl.ds((REACH - o) * block, block)],
            s_edge.at[n],
            r_edge.at[n],
            near(o),
        )
        for n, o in enumerate(NEAR)
    ]
    for c in edges:
        c.start()
    for c in loads[1:]:
        c.wait()

    cols = lax.broadcasted_iota(jnp.int32, (32, 32, 128), 1)

    def middle(p, total):
        here_in = inp[p]
        wide = here_in.astype(F32)
        xs[p, 2:34, :, 128:256] = here_in
        ahead = jnp.where(cols >= 2, pltpu.roll(wide, 2, 1), 0.0)
        xs[p, 2:34, :, 0:128] = ahead.astype(BF)
        behind = jnp.where(cols < 30, pltpu.roll(wide, 30, 1), 0.0)
        xs[p, 2:34, :, 256:384] = behind.astype(BF)
        cpad[p, 0:4] = jnp.zeros((4, 32, 128), BF)
        cpad[p, 36:40] = jnp.zeros((4, 32, 128), BF)
        here_cot = cpad[p, 4:36]
        return total + here_cot.astype(F32).reshape(128, 8, 128).sum(axis=0)

    bias8 = lax.fori_loop(0, here, middle, jnp.zeros((8, 128), F32))
    bias_here = jnp.sum(bias8, axis=0, keepdims=True)
    wacc[...] = jnp.zeros_like(wacc)

    def outer_dot(a, b):
        return lax.dot_general(
            a, b, (((0,), (0,)), ((), ())), preferred_element_type=F32
        )

    def inner(n, carry):
        p, y0 = n // 4, lax.rem(n, 4) * 8 + 2
        lhs = xs[p, pl.ds(y0, 8)].reshape(256, 384)
        rhs = jnp.concatenate(
            [cpad[p, pl.ds(y0 + 4 - 2 * a, 8)].reshape(256, 128) for a in range(3)],
            axis=1,
        )
        wacc[...] += outer_dot(lhs, rhs)
        return carry

    lax.fori_loop(0, here * 4, inner, 0)

    for a in range(3):
        for b in range(3):
            piece = w[128 * (3 * a + b) : 128 * (3 * a + b) + 128]
            wt[128 * a : 128 * a + 128, 128 * b : 128 * b + 128] = piece.T
    cols6 = lax.broadcasted_iota(jnp.int32, (6, 32, 128), 1)

    def spread_back(n, carry):
        p, y0 = n // 6, lax.rem(n, 6) * 6
        lhs = jnp.concatenate(
            [cpad[p, pl.ds(y0 + 4 - 2 * a, 6)].reshape(192, 128) for a in range(3)],
            axis=1,
        )
        got = dot(lhs, wt[...])
        z0 = got[:, 0:128].reshape(6, 32, 128)
        z1 = got[:, 128:256].reshape(6, 32, 128)
        z2 = got[:, 256:384].reshape(6, 32, 128)
        zl[p, pl.ds(y0, 6)] = z0[:, 0:16].astype(BF)
        zr[p, pl.ds(y0, 6)] = z2[:, 16:32].astype(BF)
        total = z1 + jnp.where(cols6 < 30, pltpu.roll(z0, 30, 1), 0.0)
        total = total + jnp.where(cols6 >= 2, pltpu.roll(z2, 2, 1), 0.0)
        center[p, pl.ds(y0, 6)] = total
        return carry

    lax.fori_loop(0, here * 3, spread_back, 0)
    for c in edges:
        c.wait_recv()

    r192 = rows_iota(192)
    which, deep, on = r192 // 64, lax.rem(r192 // 32, 2), lax.rem(r192, 32)
    at = 2 * which + on
    r512 = rows_iota(512)
    line, place = r512 // 16, lax.rem(r512, 16)

    def halo(p, carry):
        def info(j):
            row, c1, c2 = side_scalars(j, nb[p, j], rot[p, j], me, count, here)
            return pool[row], c1, c2, cor[p, j] > 0

        for base, first in ((0, 0), (5, 34)):
            made = jnp.zeros((192, 128), F32)
            for j, c, inside in (
                (base, 30 + at, at < 2),
                (base + 1, at - 2, (at >= 2) & (at < 34)),
                (base + 2, at - 34, at >= 34),
            ):
                strip, c1, c2, present = info(j)
                target = 32 * flip(c1, deep, 1) + flip(c2, c, 31)
                target = jnp.where(inside & present, target, -1)
                made = made + dot(onehot(target, 64), strip)
            made = made.astype(BF)
            for b in range(3):
                piece = made[64 * b : 64 * b + 64].reshape(2, 32, 128)
                xs[p, first : first + 2, :, 128 * b : 128 * b + 128] = piece
        wacc[:, 0:128] += outer_dot(
            xs[p, 0:2].reshape(64, 384), cpad[p, 4:6].reshape(64, 128)
        )
        wacc[:, 256:384] += outer_dot(
            xs[p, 34:36].reshape(64, 384), cpad[p, 34:36].reshape(64, 128)
        )
        for j, shift, lo, lane in ((3, 0, 0, 0), (4, 14, 16, 256)):
            strip, c1, c2, present = info(j)
            side = place - shift
            target = 32 * flip(c1, side, 1) + flip(c2, line, 31)
            inside = (side >= 0) & (side < 2) & present
            made = dot(onehot(jnp.where(inside, target, -1), 64), strip)
            rhs = jnp.concatenate(
                [
                    cpad[p, 6 - 2 * a : 38 - 2 * a, lo : lo + 16].reshape(512, 128)
                    for a in range(3)
                ],
                axis=1,
            )
            wacc[lane : lane + 128] += outer_dot(made.astype(BF), rhs)
            old = xs[p, 2:34, lo : lo + 16, lane : lane + 128].astype(F32)
            xs[p, 2:34, lo : lo + 16, lane : lane + 128] = (
                old + made.reshape(32, 16, 128)
            ).astype(BF)
        return carry

    lax.fori_loop(0, here, halo, 0)

    wide = wloc.shape[1] - mr
    row_t = lax.broadcasted_iota(jnp.int32, (wide, 128), 0)

    def split_bias(tail):
        b = tail[tr : tr + 1] + tail[tr + 1 : tr + 2]
        top = b.astype(BF).astype(F32)
        return jnp.where(row_t == tr, top, jnp.where(row_t == tr + 1, b - top, tail))

    def tap(t):
        a, b = t // 3, t % 3
        return wacc[128 * b : 128 * b + 128, 128 * a : 128 * a + 128]

    each = 128 // mr
    for t in range(8):
        wloc[t * each : (t + 1) * each, 0:mr] = tap(t).reshape(each, mr, 128)
    last = tap(8)
    for s in range(2 * plane):
        rows = [last[s * tr : (s + 1) * tr], bias_here]
        rows.append(jnp.zeros((wide - tr - 1, 128), F32))
        wloc[s, mr:] = jnp.concatenate(rows, axis=0)

    swap = copy(
        wloc.at[pl.ds((1 - core) * plane, plane)], core_in, s_core, r_core, mate
    )
    swap.start()

    def conv(n, carry):
        p, i0 = n // 4, lax.rem(n, 4) * 8
        lhs = jnp.concatenate(
            [xs[p, pl.ds(i0 + 2 * a, 8)].reshape(256, 384) for a in range(3)], axis=1
        )
        out[p, pl.ds(i0, 8)] = (dot(lhs, w[...]) + bias[...]).astype(BF).reshape(8, 32, 128)
        return carry

    lax.fori_loop(here * 3, here * 4, spread_back, 0)
    swap.wait_recv()

    half = (nx // 2) * ny + ny // 2

    def order(n):
        return lax.rem(n // ny + nx // 2, nx) * ny + lax.rem(lax.rem(n, ny) + ny // 2, ny)

    def p_reduce(k):
        qk, peer = peer_of(k)
        return copy(p_out.at[qk], p_in.at[k - 1], s_p.at[k - 1], r_p.at[k - 1], peer)

    def every(fun, init):
        init = lax.fori_loop(0, half, lambda n, c: fun(order(n), c), init)
        return lax.fori_loop(half + 1, plane, lambda n, c: fun(order(n), c), init)

    def p_start(k, c):
        qk = peer_of(k)[0]
        slab = wloc[core * plane + qk] + core_in[qk]
        p_out[qk, 0:mr] = slab[0:mr].astype(BF)
        p_out[qk, mr:] = split_bias(slab[mr:]).astype(BF)
        p_reduce(k).start()
        return c

    every(p_start, 0)
    lax.fori_loop(here * 4, here * 6, spread_back, 0)

    def last_two(step, c):
        return jnp.where(c >= 30, step + c - 30, -1)

    def first_two(step, c):
        return jnp.where(c < 2, step + 14 + c, -1)

    def turn_back(p, carry):
        def back(j, target_of, piece):
            row, c1, c2 = side_scalars(j, nb[p, j], rot[p, j], me, count, here)
            target = target_of(flip(c1, depth, 1), flip(c2, along, 31))
            target = jnp.where(cor[p, j] > 0, target, -1)
            spots[p * 8 + j] = row
            tst[p * 8 + j] = dot(onehot(target, piece.shape[0]), piece)

        for base, lo in ((0, 0), (5, 34)):
            mid = center[p, lo : lo + 2].reshape(64, 128).astype(BF)
            ends = zl[p, lo : lo + 2].reshape(32, 128)
            back(base, lambda r, c: last_two(16 * r, c), ends)
            back(base + 1, lambda r, c: 32 * r + c, mid)
            ends = zr[p, lo : lo + 2].reshape(32, 128)
            back(base + 2, lambda r, c: first_two(16 * r, c), ends)
        back(3, lambda c, i: 16 * i + c, zl[p, 2:34].reshape(512, 128))
        back(4, lambda c, i: 16 * i + 14 + c, zr[p, 2:34].reshape(512, 128))
        return carry

    def gather_terms(s, carry):
        total = jnp.zeros((64, 128), F32)
        for n in range(here * 8):
            total = total + jnp.where(spots[n] == s, 1.0, 0.0) * tst[n]
        terms[s] = total.astype(BF)
        return carry

    lax.fori_loop(0, here, turn_back, 0)
    lax.fori_loop(0, 5 * block, gather_terms, 0)

    def p_add(k, c):
        p_reduce(k).wait_recv()
        return c + p_in[k - 1].astype(F32)

    z_all[z] = every(p_add, wloc[core * plane + q] + core_in[q])

    def z_gather(k):
        return copy(z_all.at[z], z_all.at[z], s_z.at[k - 1], r_z.at[k - 1], z_peer(k))

    for k in range(1, nz):
        z_gather(k).start()
    backs = [
        copy(
            terms.at[pl.ds((REACH + o) * block, block)],
            arr.at[n],
            s_term.at[n],
            r_term.at[n],
            near(o),
        )
        for n, o in enumerate(NEAR)
    ]
    for c in backs:
        c.start()

    lax.fori_loop(0, 4 * here, conv, 0)
    stores = [pltpu.make_async_copy(out, out_o, s_store.at[0])]
    stores[0].start()
    for k in range(1, nz):
        z_gather(k).wait_recv()
    slab = z_all[0]
    for n in range(1, nz):
        slab = slab + z_all[n]
    slab = slab * factor
    spot = core * plane + q
    fin[spot, 0:mr] = slab[0:mr].astype(BF)
    fin[spot, mr:] = split_bias(slab[mr:]).astype(BF)

    def p_gather(k):
        return copy(fin.at[spot], fin.at[spot], s_g.at[k - 1], r_g.at[k - 1], peer_of(k)[1])

    def g_start(k, c):
        p_gather(k).start()
        return c

    every(g_start, 0)
    for c in backs:
        c.wait_recv()

    def finish(p, carry):
        def pieces_of(slot):
            found = [terms[REACH * block + p * 4 + slot]]
            return found + [arr[n, p * 4 + slot] for n in range(len(NEAR))]

        def arrived(slot):
            total = jnp.zeros((64, 128), F32)
            for piece in pieces_of(slot):
                total = total + piece.astype(F32)
            return total.reshape(2, 32, 128)

        top, bottom = arrived(0), arrived(1)
        for slot, shift, lo in ((2, 0, 0), (3, 14, 16)):
            at_col = place - shift
            inside = (at_col >= 0) & (at_col < 2)
            spread = onehot(jnp.where(inside, 32 * at_col + line, -1), 64)
            made = jnp.zeros((512, 128), F32)
            for piece in pieces_of(slot):
                made = made + dot(spread, piece)
            total = center[p, 2:34, lo : lo + 16] + made.reshape(32, 16, 128)
            upper = total[0:2] + top[:, lo : lo + 16]
            lower = total[30:32] + bottom[:, lo : lo + 16]
            ingrad[p, 0:2, lo : lo + 16] = upper.astype(BF)
            ingrad[p, 2:30, lo : lo + 16] = total[2:30].astype(BF)
            ingrad[p, 30:32, lo : lo + 16] = lower.astype(BF)
        return carry

    lax.fori_loop(0, here, finish, 0)
    stores.append(pltpu.make_async_copy(ingrad, ingrad_o, s_store.at[1]))
    stores[1].start()

    def g_wait(k, c):
        p_gather(k).wait_recv()
        return c

    every(g_wait, 0)
    mine = pl.ds(core * plane, plane)
    hand = copy(fin.at[mine], fin_o.at[mine], s_last, r_last, mate)
    hand.start()
    stores.append(pltpu.make_async_copy(fin.at[mine], fin_o.at[mine], s_store.at[2]))
    stores[2].start()

    def sent(k, c):
        p_reduce(k).wait_send()
        p_gather(k).wait_send()
        return c

    every(sent, 0)
    for c in edges + backs + [swap]:
        c.wait_send()
    for k in range(1, nz):
        z_gather(k).wait_send()
    for c in stores:
        c.wait()
    hand.wait()


def write_kernel(
    mr, tr, out, ingrad, fin_o, out_o, ingrad_o, wgrad_o, bgrad, fin, held, wide, sems
):
    here = out.shape[0]
    load = pltpu.make_async_copy(fin_o, fin, sems.at[0])
    load.start()
    loads, stores = [], []
    for p in range(here):
        for n, (src, dst) in enumerate(((out, out_o), (ingrad, ingrad_o))):
            at = 2 * p + n
            loads.append(
                pltpu.make_async_copy(src.at[p], held.at[at], sems.at[2 + 2 * at])
            )
            stores.append(
                pltpu.make_async_copy(held.at[at], dst.at[p], sems.at[3 + 2 * at])
            )
            loads[-1].start()
    load.wait()
    slabs = fin.shape[0]
    wide[0:1024] = fin[:, 0:mr].astype(F32).reshape(1024, 128)
    for s in range(slabs):
        tail = fin[s, mr:].astype(F32)
        wide[1024 + tr * s : 1024 + tr * (s + 1)] = tail[0:tr]
    stores.append(pltpu.make_async_copy(wide, wgrad_o, sems.at[1]))
    stores[-1].start()
    tail = fin[0, mr:].astype(F32)
    bgrad[...] = tail[tr : tr + 1] + tail[tr + 1 : tr + 2]
    for c, d in zip(loads, stores):
        c.wait()
        d.start()
    for c in stores:
        c.wait()


def body(count, inputs, cotangent, weights, bias_vector, neighbours, rotations, corners):
    here, length, _, chans = inputs.shape
    sizes = TORUS[count]
    nz, nx, ny = sizes
    plane = nx * ny
    factor = 1.0 / (length * math.sqrt(here * count))
    block = here * 4
    hbm = pl.BlockSpec(memory_space=pltpu.HBM)
    vmem = pl.BlockSpec(memory_space=pltpu.VMEM)
    dma = pltpu.SemaphoreType.DMA
    mr, tr = 1024 // (2 * plane), 128 // (2 * plane)
    rows = mr + -(-(tr + 2) // 8) * 8
    near = len(NEAR)
    wires = [near, near, None, plane - 1, nz - 1, plane - 1, None]
    outputs, input_grad, fin = pl.pallas_call(
        functools.partial(main_kernel, sizes, factor),
        out_shape=(
            jax.ShapeDtypeStruct(inputs.shape, BF),
            jax.ShapeDtypeStruct(inputs.shape, BF),
            jax.ShapeDtypeStruct((2 * plane, rows, chans), BF),
        ),
        in_specs=[hbm] * 7,
        out_specs=(hbm,) * 3,
        scratch_shapes=[
            pltpu.VMEM(inputs.shape, BF),
            pltpu.VMEM(inputs.shape, BF),
            pltpu.VMEM((2 * plane, rows, chans), BF),
            pltpu.SMEM((here, 8), jnp.int32),
            pltpu.SMEM((here, 8), jnp.int32),
            pltpu.SMEM((here, 8), jnp.int32),
            pltpu.VMEM(inputs.shape, BF),
            pltpu.VMEM((9 * chans, chans), BF),
            pltpu.VMEM((1, chans), F32),
            pltpu.VMEM((3 * chans, 3 * chans), BF),
            pltpu.VMEM((5 * block, 64, chans), BF),
            pltpu.VMEM((here, 36, 32, chans), F32),
            pltpu.VMEM((here, 36, 16, chans), BF),
            pltpu.VMEM((here, 36, 16, chans), BF),
            pltpu.VMEM((near, block, 64, chans), BF),
            pltpu.VMEM((5 * block, 64, chans), BF),
            pltpu.VMEM((here * 8, 64, chans), F32),
            pltpu.SMEM((here * 8,), jnp.int32),
            pltpu.VMEM((here, 36, 32, 3 * chans), BF),
            pltpu.VMEM((here, 40, 32, chans), BF),
            pltpu.VMEM((3 * chans, 3 * chans), F32),
            pltpu.VMEM((2 * plane, rows, chans), F32),
            pltpu.VMEM((plane, rows, chans), F32),
            pltpu.VMEM((plane, rows, chans), BF),
            pltpu.VMEM((plane - 1, rows, chans), BF),
            pltpu.VMEM((nz, rows, chans), F32),
            dma((6 + here,)),
            dma((3,)),
        ]
        + [dma if n is None else dma((n,)) for n in wires for _ in range(2)],
        compiler_params=pltpu.CompilerParams(
            collective_id=0, has_side_effects=True, vmem_limit_bytes=56 * 2**20
        ),
    )(
        neighbours,
        rotations,
        corners,
        inputs,
        cotangent,
        weights.reshape(9 * chans, chans),
        bias_vector.reshape(1, chans),
    )
    outputs, input_grad, weight_grad, bias_grad = pl.pallas_call(
        functools.partial(write_kernel, mr, tr),
        out_shape=(
            jax.ShapeDtypeStruct(inputs.shape, BF),
            jax.ShapeDtypeStruct(inputs.shape, BF),
            jax.ShapeDtypeStruct((9 * chans, chans), F32),
            jax.ShapeDtypeStruct((1, chans), F32),
        ),
        in_specs=[hbm] * 3,
        out_specs=(hbm, hbm, hbm, vmem),
        scratch_shapes=[
            pltpu.VMEM((2 * plane, rows, chans), BF),
            pltpu.VMEM((2 * here, length, length, chans), BF),
            pltpu.VMEM((9 * chans, chans), F32),
            dma((2 + 4 * here,)),
        ],
        compiler_params=pltpu.CompilerParams(vmem_limit_bytes=56 * 2**20),
    )(outputs, input_grad, fin)
    return (
        outputs,
        input_grad,
        weight_grad.reshape(weights.shape),
        bias_grad.reshape(bias_vector.shape),
    )


def solution(mesh):
    in_specs = (
        P("patch", None, None, None),
        P("patch", None, None, None),
        P(),
        P(),
        P("patch", None),
        P("patch", None),
        P("patch", None),
    )
    out_specs = (P("patch", None, None, None), P("patch", None, None, None), P(), P())
    return jax.shard_map(
        functools.partial(body, mesh.shape["patch"]),
        mesh=mesh,
        in_specs=in_specs,
        out_specs=out_specs,
        check_vma=False,
    )
```

```python
import functools
import math

import jax
import jax.numpy as jnp
from jax import lax
from jax.experimental import pallas as pl
from jax.experimental.pallas import tpu as pltpu
from jax.sharding import PartitionSpec as P

REACH = 2
NEAR = (-2, -1, 1, 2)
MESH = pl.DeviceIdType.MESH
BF = jnp.bfloat16
F32 = jnp.float32
SIDE_TABLE = (
    ((0, 0), (3, 1), (1, 3), (2, 2)),
    ((1, 0), (2, 1), (0, 3), (3, 2)),
    ((2, 0), (0, 2), (3, 3), (1, 1)),
    ((3, 0), (1, 2), (2, 3), (0, 1)),
)
WANTED = (1, 1, 1, 3, 2, 0, 0, 0)
TORUS = {512: (8, 4, 8), 16: (2, 2, 2)}


def pick(k, values):
    out = jnp.int32(values[3])
    for i in (2, 1, 0):
        out = jnp.where(k == i, jnp.int32(values[i]), out)
    return out


def side_scalars(j, nb, rot, me, count, here):
    owner = nb // here
    off = lax.rem(owner - me + REACH + count, count)
    place = jnp.minimum(off, 2 * REACH) * here + (nb - owner * here)
    table = SIDE_TABLE[WANTED[j]]
    slot = pick(rot, [table[k][0] for k in range(4)])
    c1 = pick(rot, [table[k][1] & 1 for k in range(4)])
    c2 = pick(rot, [table[k][1] >> 1 for k in range(4)])
    return place * 4 + slot, c1, c2


def onehot(target, width):
    rows = target.shape[0]
    lanes = lax.broadcasted_iota(jnp.int32, (rows, width), 1)
    return jnp.where(lanes == target, 1.0, 0.0).astype(BF)


def rows_iota(rows):
    return lax.broadcasted_iota(jnp.int32, (rows, 1), 0)


def flip(c, x, last):
    return last * c + (1 - 2 * c) * x


def dot(a, b):
    return jnp.dot(a, b, preferred_element_type=F32)


def main_kernel(
    sizes,
    factor,
    nb_in,
    rot_in,
    cor_in,
    inp_in,
    cot_in,
    w_in,
    bias_in,
    out_o,
    ingrad_o,
    fin_o,
    out,
    ingrad,
    fin,
    nb,
    rot,
    cor,
    inp,
    w,
    bias,
    wt,
    pool,
    center,
    zl,
    zr,
    arr,
    terms,
    tst,
    spots,
    xs,
    cpad,
    wacc,
    wloc,
    core_in,
    p_out,
    p_in,
    z_all,
    s_load,
    s_store,
    s_edge,
    r_edge,
    s_term,
    r_term,
    s_core,
    r_core,
    s_p,
    r_p,
    s_z,
    r_z,
    s_g,
    r_g,
    s_last,
    r_last,
):
    nz, nx, ny = sizes
    count = nz * nx * ny * 2
    plane = nx * ny
    me = lax.axis_index("patch")
    here = inp.shape[0]
    loads = [
        pltpu.make_async_copy(src, dst, s_load.at[n])
        for n, (src, dst) in enumerate(
            [(inp_in, inp), (nb_in, nb), (rot_in, rot), (cor_in, cor)]
            + [(w_in, w), (bias_in, bias)]
            + [(cot_in.at[p], cpad.at[p, 4:36]) for p in range(here)]
        )
    ]
    for c in loads:
        c.start()
    core = lax.rem(me, 2)
    y = lax.rem(me // 2, ny)
    x = lax.rem(me // (2 * ny), nx)
    z = me // (2 * ny * nx)
    u, u_step = y + core * (z - y), 2 + core * (2 * plane - 2)
    v, v_step = z + core * (y - z), 2 * plane + core * (2 - 2 * plane)
    q = x * ny + u
    mate = me + 1 - 2 * core
    block = here * 4
    mr, tr = 1024 // (2 * plane), 128 // (2 * plane)

    def peer_of(k):
        xk, uk = lax.rem(x + k // ny, nx), lax.rem(u + lax.rem(k, ny), ny)
        return xk * ny + uk, me + 2 * ny * (xk - x) + u_step * (uk - u)

    def v_peer(k):
        return me + v_step * (lax.rem(v + k, nz) - v)

    def near(o):
        return lax.rem(me + o + count, count)

    def copy(src, dst, send, recv, to):
        return pltpu.make_async_remote_copy(
            src_ref=src,
            dst_ref=dst,
            send_sem=send,
            recv_sem=recv,
            device_id=(to,),
            device_id_type=MESH,
        )

    barrier = pltpu.get_barrier_semaphore()

    def greet(peer):
        pl.semaphore_signal(barrier, inc=1, device_id=(peer,), device_id_type=MESH)

    def greet_plane(k, carry):
        greet(peer_of(k)[1])
        return carry

    for k in range(1, nz):
        greet(v_peer(k))
    lax.fori_loop(1, plane, greet_plane, 0)
    for o in NEAR:
        greet(near(o))
    greet(mate)

    r64 = rows_iota(64)
    depth, along = r64 // 32, lax.rem(r64, 32)
    own = REACH * block
    loads[0].wait()

    def pack(p, carry):
        pool[own + p * 4] = inp[p, 0:2].reshape(64, 128)
        pool[own + p * 4 + 1] = inp[p, 30:32].reshape(64, 128)
        left = inp[p, :, 0:16, :].reshape(512, 128)
        pool[own + p * 4 + 2] = dot(onehot(along * 16 + depth, 512), left).astype(BF)
        right = inp[p, :, 16:32, :].reshape(512, 128)
        right = dot(onehot(along * 16 + depth + 14, 512), right)
        pool[own + p * 4 + 3] = right.astype(BF)
        return carry

    lax.fori_loop(0, here, pack, 0)
    pl.semaphore_wait(barrier, nz - 1 + plane - 1 + len(NEAR) + 1)
    edges = [
        copy(
            pool.at[pl.ds(own, block)],
            pool.at[pl.ds((REACH - o) * block, block)],
            s_edge.at[n],
            r_edge.at[n],
            near(o),
        )
        for n, o in enumerate(NEAR)
    ]
    for c in edges:
        c.start()
    for c in loads[1:]:
        c.wait()

    cols = lax.broadcasted_iota(jnp.int32, (32, 32, 128), 1)

    def middle(p, total):
        here_in = inp[p]
        wide = here_in.astype(F32)
        xs[p, 2:34, :, 128:256] = here_in
        ahead = jnp.where(cols >= 2, pltpu.roll(wide, 2, 1), 0.0)
        xs[p, 2:34, :, 0:128] = ahead.astype(BF)
        behind = jnp.where(cols < 30, pltpu.roll(wide, 30, 1), 0.0)
        xs[p, 2:34, :, 256:384] = behind.astype(BF)
        cpad[p, 0:4] = jnp.zeros((4, 32, 128), BF)
        cpad[p, 36:40] = jnp.zeros((4, 32, 128), BF)
        here_cot = cpad[p, 4:36]
        return total + here_cot.astype(F32).reshape(128, 8, 128).sum(axis=0)

    bias8 = lax.fori_loop(0, here, middle, jnp.zeros((8, 128), F32))
    bias_here = jnp.sum(bias8, axis=0, keepdims=True)
    wacc[...] = jnp.zeros_like(wacc)

    def outer_dot(a, b):
        return lax.dot_general(
            a, b, (((0,), (0,)), ((), ())), preferred_element_type=F32
        )

    def inner(n, carry):
        p, y0 = n // 4, lax.rem(n, 4) * 8 + 2
        lhs = xs[p, pl.ds(y0, 8)].reshape(256, 384)
        rhs = jnp.concatenate(
            [cpad[p, pl.ds(y0 + 4 - 2 * a, 8)].reshape(256, 128) for a in range(3)],
            axis=1,
        )
        wacc[...] += outer_dot(lhs, rhs)
        return carry

    lax.fori_loop(0, here * 4, inner, 0)

    for a in range(3):
        for b in range(3):
            piece = w[128 * (3 * a + b) : 128 * (3 * a + b) + 128]
            wt[128 * a : 128 * a + 128, 128 * b : 128 * b + 128] = piece.T
    cols6 = lax.broadcasted_iota(jnp.int32, (6, 32, 128), 1)

    def spread_back(n, carry):
        p, y0 = n // 6, lax.rem(n, 6) * 6
        lhs = jnp.concatenate(
            [cpad[p, pl.ds(y0 + 4 - 2 * a, 6)].reshape(192, 128) for a in range(3)],
            axis=1,
        )
        got = dot(lhs, wt[...])
        z0 = got[:, 0:128].reshape(6, 32, 128)
        z1 = got[:, 128:256].reshape(6, 32, 128)
        z2 = got[:, 256:384].reshape(6, 32, 128)
        zl[p, pl.ds(y0, 6)] = z0[:, 0:16].astype(BF)
        zr[p, pl.ds(y0, 6)] = z2[:, 16:32].astype(BF)
        total = z1 + jnp.where(cols6 < 30, pltpu.roll(z0, 30, 1), 0.0)
        total = total + jnp.where(cols6 >= 2, pltpu.roll(z2, 2, 1), 0.0)
        center[p, pl.ds(y0, 6)] = total
        return carry

    lax.fori_loop(0, here * 3, spread_back, 0)
    for c in edges:
        c.wait_recv()

    r192 = rows_iota(192)
    which, deep, on = r192 // 64, lax.rem(r192 // 32, 2), lax.rem(r192, 32)
    at = 2 * which + on
    r512 = rows_iota(512)
    line, place = r512 // 16, lax.rem(r512, 16)

    def halo(p, carry):
        def info(j):
            row, c1, c2 = side_scalars(j, nb[p, j], rot[p, j], me, count, here)
            return pool[row], c1, c2, cor[p, j] > 0

        for base, first in ((0, 0), (5, 34)):
            made = jnp.zeros((192, 128), F32)
            for j, c, inside in (
                (base, 30 + at, at < 2),
                (base + 1, at - 2, (at >= 2) & (at < 34)),
                (base + 2, at - 34, at >= 34),
            ):
                strip, c1, c2, present = info(j)
                target = 32 * flip(c1, deep, 1) + flip(c2, c, 31)
                target = jnp.where(inside & present, target, -1)
                made = made + dot(onehot(target, 64), strip)
            made = made.astype(BF)
            for b in range(3):
                piece = made[64 * b : 64 * b + 64].reshape(2, 32, 128)
                xs[p, first : first + 2, :, 128 * b : 128 * b + 128] = piece
        wacc[:, 0:128] += outer_dot(
            xs[p, 0:2].reshape(64, 384), cpad[p, 4:6].reshape(64, 128)
        )
        wacc[:, 256:384] += outer_dot(
            xs[p, 34:36].reshape(64, 384), cpad[p, 34:36].reshape(64, 128)
        )
        for j, shift, lo, lane in ((3, 0, 0, 0), (4, 14, 16, 256)):
            strip, c1, c2, present = info(j)
            side = place - shift
            target = 32 * flip(c1, side, 1) + flip(c2, line, 31)
            inside = (side >= 0) & (side < 2) & present
            made = dot(onehot(jnp.where(inside, target, -1), 64), strip)
            rhs = jnp.concatenate(
                [
                    cpad[p, 6 - 2 * a : 38 - 2 * a, lo : lo + 16].reshape(512, 128)
                    for a in range(3)
                ],
                axis=1,
            )
            wacc[lane : lane + 128] += outer_dot(made.astype(BF), rhs)
            old = xs[p, 2:34, lo : lo + 16, lane : lane + 128].astype(F32)
            xs[p, 2:34, lo : lo + 16, lane : lane + 128] = (
                old + made.reshape(32, 16, 128)
            ).astype(BF)
        return carry

    lax.fori_loop(0, here, halo, 0)

    wide = wloc.shape[1] - mr
    row_t = lax.broadcasted_iota(jnp.int32, (wide, 128), 0)

    def split_bias(tail):
        b = tail[tr : tr + 1] + tail[tr + 1 : tr + 2]
        top = b.astype(BF).astype(F32)
        return jnp.where(row_t == tr, top, jnp.where(row_t == tr + 1, b - top, tail))

    def tap(t):
        a, b = t // 3, t % 3
        return wacc[128 * b : 128 * b + 128, 128 * a : 128 * a + 128]

    each = 128 // mr
    for t in range(8):
        wloc[t * each : (t + 1) * each, 0:mr] = tap(t).reshape(each, mr, 128)
    last = tap(8)
    for s in range(2 * plane):
        rows = [last[s * tr : (s + 1) * tr], bias_here]
        rows.append(jnp.zeros((wide - tr - 1, 128), F32))
        wloc[s, mr:] = jnp.concatenate(rows, axis=0)

    swap = copy(
        wloc.at[pl.ds((1 - core) * plane, plane)], core_in, s_core, r_core, mate
    )
    swap.start()

    def conv(n, carry):
        p, i0 = n // 4, lax.rem(n, 4) * 8
        lhs = jnp.concatenate(
            [xs[p, pl.ds(i0 + 2 * a, 8)].reshape(256, 384) for a in range(3)], axis=1
        )
        out[p, pl.ds(i0, 8)] = (dot(lhs, w[...]) + bias[...]).astype(BF).reshape(8, 32, 128)
        return carry

    lax.fori_loop(here * 3, here * 4, spread_back, 0)
    swap.wait_recv()

    half = (nx // 2) * ny + ny // 2

    def order(n):
        return lax.rem(n // ny + nx // 2, nx) * ny + lax.rem(lax.rem(n, ny) + ny // 2, ny)

    def p_reduce(k):
        qk, peer = peer_of(k)
        return copy(p_out.at[qk], p_in.at[k - 1], s_p.at[k - 1], r_p.at[k - 1], peer)

    def every(fun, init):
        init = lax.fori_loop(0, half, lambda n, c: fun(order(n), c), init)
        return lax.fori_loop(half + 1, plane, lambda n, c: fun(order(n), c), init)

    def p_start(k, c):
        qk = peer_of(k)[0]
        slab = wloc[core * plane + qk] + core_in[qk]
        p_out[qk, 0:mr] = slab[0:mr].astype(BF)
        p_out[qk, mr:] = split_bias(slab[mr:]).astype(BF)
        p_reduce(k).start()
        return c

    every(p_start, 0)
    lax.fori_loop(here * 4, here * 6, spread_back, 0)

    def last_two(step, c):
        return jnp.where(c >= 30, step + c - 30, -1)

    def first_two(step, c):
        return jnp.where(c < 2, step + 14 + c, -1)

    def turn_back(p, carry):
        def back(j, target_of, piece):
            row, c1, c2 = side_scalars(j, nb[p, j], rot[p, j], me, count, here)
            target = target_of(flip(c1, depth, 1), flip(c2, along, 31))
            target = jnp.where(cor[p, j] > 0, target, -1)
            spots[p * 8 + j] = row
            tst[p * 8 + j] = dot(onehot(target, piece.shape[0]), piece)

        for base, lo in ((0, 0), (5, 34)):
            mid = center[p, lo : lo + 2].reshape(64, 128).astype(BF)
            ends = zl[p, lo : lo + 2].reshape(32, 128)
            back(base, lambda r, c: last_two(16 * r, c), ends)
            back(base + 1, lambda r, c: 32 * r + c, mid)
            ends = zr[p, lo : lo + 2].reshape(32, 128)
            back(base + 2, lambda r, c: first_two(16 * r, c), ends)
        back(3, lambda c, i: 16 * i + c, zl[p, 2:34].reshape(512, 128))
        back(4, lambda c, i: 16 * i + 14 + c, zr[p, 2:34].reshape(512, 128))
        return carry

    def gather_terms(s, carry):
        total = jnp.zeros((64, 128), F32)
        for n in range(here * 8):
            total = total + jnp.where(spots[n] == s, 1.0, 0.0) * tst[n]
        terms[s] = total.astype(BF)
        return carry

    lax.fori_loop(0, here, turn_back, 0)
    lax.fori_loop(0, 5 * block, gather_terms, 0)

    def p_add(k, c):
        p_reduce(k).wait_recv()
        return c + p_in[k - 1].astype(F32)

    z_all[v] = every(p_add, wloc[core * plane + q] + core_in[q])

    def z_gather(k):
        return copy(z_all.at[v], z_all.at[v], s_z.at[k - 1], r_z.at[k - 1], v_peer(k))

    for k in range(1, nz):
        z_gather(k).start()
    backs = [
        copy(
            terms.at[pl.ds((REACH + o) * block, block)],
            arr.at[n],
            s_term.at[n],
            r_term.at[n],
            near(o),
        )
        for n, o in enumerate(NEAR)
    ]
    for c in backs:
        c.start()

    lax.fori_loop(0, 4 * here, conv, 0)
    stores = [pltpu.make_async_copy(out, out_o, s_store.at[0])]
    stores[0].start()
    for k in range(1, nz):
        z_gather(k).wait_recv()
    slab = z_all[0]
    for n in range(1, nz):
        slab = slab + z_all[n]
    slab = slab * factor
    spot = core * plane + q
    fin[spot, 0:mr] = slab[0:mr].astype(BF)
    fin[spot, mr:] = split_bias(slab[mr:]).astype(BF)

    def p_gather(k):
        return copy(fin.at[spot], fin.at[spot], s_g.at[k - 1], r_g.at[k - 1], peer_of(k)[1])

    def g_start(k, c):
        p_gather(k).start()
        return c

    every(g_start, 0)
    for c in backs:
        c.wait_recv()

    def finish(p, carry):
        def pieces_of(slot):
            found = [terms[REACH * block + p * 4 + slot]]
            return found + [arr[n, p * 4 + slot] for n in range(len(NEAR))]

        def arrived(slot):
            total = jnp.zeros((64, 128), F32)
            for piece in pieces_of(slot):
                total = total + piece.astype(F32)
            return total.reshape(2, 32, 128)

        top, bottom = arrived(0), arrived(1)
        for slot, shift, lo in ((2, 0, 0), (3, 14, 16)):
            at_col = place - shift
            inside = (at_col >= 0) & (at_col < 2)
            spread = onehot(jnp.where(inside, 32 * at_col + line, -1), 64)
            made = jnp.zeros((512, 128), F32)
            for piece in pieces_of(slot):
                made = made + dot(spread, piece)
            total = center[p, 2:34, lo : lo + 16] + made.reshape(32, 16, 128)
            upper = total[0:2] + top[:, lo : lo + 16]
            lower = total[30:32] + bottom[:, lo : lo + 16]
            ingrad[p, 0:2, lo : lo + 16] = upper.astype(BF)
            ingrad[p, 2:30, lo : lo + 16] = total[2:30].astype(BF)
            ingrad[p, 30:32, lo : lo + 16] = lower.astype(BF)
        return carry

    lax.fori_loop(0, here, finish, 0)
    stores.append(pltpu.make_async_copy(ingrad, ingrad_o, s_store.at[1]))
    stores[1].start()

    def g_wait(k, c):
        p_gather(k).wait_recv()
        return c

    every(g_wait, 0)
    mine = pl.ds(core * plane, plane)
    hand = copy(fin.at[mine], fin_o.at[mine], s_last, r_last, mate)
    hand.start()
    stores.append(pltpu.make_async_copy(fin.at[mine], fin_o.at[mine], s_store.at[2]))
    stores[2].start()

    def sent(k, c):
        p_reduce(k).wait_send()
        p_gather(k).wait_send()
        return c

    every(sent, 0)
    for c in edges + backs + [swap]:
        c.wait_send()
    for k in range(1, nz):
        z_gather(k).wait_send()
    for c in stores:
        c.wait()
    hand.wait()


def write_kernel(
    mr, tr, out, ingrad, fin_o, out_o, ingrad_o, wgrad_o, bgrad, fin, held, wide, sems
):
    here = out.shape[0]
    load = pltpu.make_async_copy(fin_o, fin, sems.at[0])
    load.start()
    loads, stores = [], []
    for p in range(here):
        for n, (src, dst) in enumerate(((out, out_o), (ingrad, ingrad_o))):
            at = 2 * p + n
            loads.append(
                pltpu.make_async_copy(src.at[p], held.at[at], sems.at[2 + 2 * at])
            )
            stores.append(
                pltpu.make_async_copy(held.at[at], dst.at[p], sems.at[3 + 2 * at])
            )
            loads[-1].start()
    load.wait()
    slabs = fin.shape[0]
    wide[0:1024] = fin[:, 0:mr].astype(F32).reshape(1024, 128)
    for s in range(slabs):
        tail = fin[s, mr:].astype(F32)
        wide[1024 + tr * s : 1024 + tr * (s + 1)] = tail[0:tr]
    stores.append(pltpu.make_async_copy(wide, wgrad_o, sems.at[1]))
    stores[-1].start()
    tail = fin[0, mr:].astype(F32)
    bgrad[...] = tail[tr : tr + 1] + tail[tr + 1 : tr + 2]
    for c, d in zip(loads, stores):
        c.wait()
        d.start()
    for c in stores:
        c.wait()


def body(count, inputs, cotangent, weights, bias_vector, neighbours, rotations, corners):
    here, length, _, chans = inputs.shape
    sizes = TORUS[count]
    nz, nx, ny = sizes
    plane = nx * ny
    factor = 1.0 / (length * math.sqrt(here * count))
    block = here * 4
    hbm = pl.BlockSpec(memory_space=pltpu.HBM)
    vmem = pl.BlockSpec(memory_space=pltpu.VMEM)
    dma = pltpu.SemaphoreType.DMA
    mr, tr = 1024 // (2 * plane), 128 // (2 * plane)
    rows = mr + -(-(tr + 2) // 8) * 8
    near = len(NEAR)
    wires = [near, near, None, plane - 1, nz - 1, plane - 1, None]
    outputs, input_grad, fin = pl.pallas_call(
        functools.partial(main_kernel, sizes, factor),
        out_shape=(
            jax.ShapeDtypeStruct(inputs.shape, BF),
            jax.ShapeDtypeStruct(inputs.shape, BF),
            jax.ShapeDtypeStruct((2 * plane, rows, chans), BF),
        ),
        in_specs=[hbm] * 7,
        out_specs=(hbm,) * 3,
        scratch_shapes=[
            pltpu.VMEM(inputs.shape, BF),
            pltpu.VMEM(inputs.shape, BF),
            pltpu.VMEM((2 * plane, rows, chans), BF),
            pltpu.SMEM((here, 8), jnp.int32),
            pltpu.SMEM((here, 8), jnp.int32),
            pltpu.SMEM((here, 8), jnp.int32),
            pltpu.VMEM(inputs.shape, BF),
            pltpu.VMEM((9 * chans, chans), BF),
            pltpu.VMEM((1, chans), F32),
            pltpu.VMEM((3 * chans, 3 * chans), BF),
            pltpu.VMEM((5 * block, 64, chans), BF),
            pltpu.VMEM((here, 36, 32, chans), F32),
            pltpu.VMEM((here, 36, 16, chans), BF),
            pltpu.VMEM((here, 36, 16, chans), BF),
            pltpu.VMEM((near, block, 64, chans), BF),
            pltpu.VMEM((5 * block, 64, chans), BF),
            pltpu.VMEM((here * 8, 64, chans), F32),
            pltpu.SMEM((here * 8,), jnp.int32),
            pltpu.VMEM((here, 36, 32, 3 * chans), BF),
            pltpu.VMEM((here, 40, 32, chans), BF),
            pltpu.VMEM((3 * chans, 3 * chans), F32),
            pltpu.VMEM((2 * plane, rows, chans), F32),
            pltpu.VMEM((plane, rows, chans), F32),
            pltpu.VMEM((plane, rows, chans), BF),
            pltpu.VMEM((plane - 1, rows, chans), BF),
            pltpu.VMEM((nz, rows, chans), F32),
            dma((6 + here,)),
            dma((3,)),
        ]
        + [dma if n is None else dma((n,)) for n in wires for _ in range(2)],
        compiler_params=pltpu.CompilerParams(
            collective_id=0, has_side_effects=True, vmem_limit_bytes=56 * 2**20
        ),
    )(
        neighbours,
        rotations,
        corners,
        inputs,
        cotangent,
        weights.reshape(9 * chans, chans),
        bias_vector.reshape(1, chans),
    )
    outputs, input_grad, weight_grad, bias_grad = pl.pallas_call(
        functools.partial(write_kernel, mr, tr),
        out_shape=(
            jax.ShapeDtypeStruct(inputs.shape, BF),
            jax.ShapeDtypeStruct(inputs.shape, BF),
            jax.ShapeDtypeStruct((9 * chans, chans), F32),
            jax.ShapeDtypeStruct((1, chans), F32),
        ),
        in_specs=[hbm] * 3,
        out_specs=(hbm, hbm, hbm, vmem),
        scratch_shapes=[
            pltpu.VMEM((2 * plane, rows, chans), BF),
            pltpu.VMEM((2 * here, length, length, chans), BF),
            pltpu.VMEM((9 * chans, chans), F32),
            dma((2 + 4 * here,)),
        ],
        compiler_params=pltpu.CompilerParams(vmem_limit_bytes=56 * 2**20),
    )(outputs, input_grad, fin)
    return (
        outputs,
        input_grad,
        weight_grad.reshape(weights.shape),
        bias_grad.reshape(bias_vector.shape),
    )


def solution(mesh):
    in_specs = (
        P("patch", None, None, None),
        P("patch", None, None, None),
        P(),
        P(),
        P("patch", None),
        P("patch", None),
        P("patch", None),
    )
    out_specs = (P("patch", None, None, None), P("patch", None, None, None), P(), P())
    return jax.shard_map(
        functools.partial(body, mesh.shape["patch"]),
        mesh=mesh,
        in_specs=in_specs,
        out_specs=out_specs,
        check_vma=False,
    )
```

```python
import functools
import math

import jax
import jax.numpy as jnp
from jax import lax
from jax.experimental import pallas as pl
from jax.experimental.pallas import tpu as pltpu
from jax.sharding import PartitionSpec as P

REACH = 2
NEAR = (-2, -1, 1, 2)
MESH = pl.DeviceIdType.MESH
BF = jnp.bfloat16
F32 = jnp.float32
SIDE_TABLE = (
    ((0, 0), (3, 1), (1, 3), (2, 2)),
    ((1, 0), (2, 1), (0, 3), (3, 2)),
    ((2, 0), (0, 2), (3, 3), (1, 1)),
    ((3, 0), (1, 2), (2, 3), (0, 1)),
)
WANTED = (1, 1, 1, 3, 2, 0, 0, 0)
TORUS = {512: (8, 4, 8), 16: (2, 2, 2)}


def pick(k, values):
    out = jnp.int32(values[3])
    for i in (2, 1, 0):
        out = jnp.where(k == i, jnp.int32(values[i]), out)
    return out


def side_scalars(j, nb, rot, me, count, here):
    owner = nb // here
    off = lax.rem(owner - me + REACH + count, count)
    place = jnp.minimum(off, 2 * REACH) * here + (nb - owner * here)
    table = SIDE_TABLE[WANTED[j]]
    slot = pick(rot, [table[k][0] for k in range(4)])
    c1 = pick(rot, [table[k][1] & 1 for k in range(4)])
    c2 = pick(rot, [table[k][1] >> 1 for k in range(4)])
    return place * 4 + slot, c1, c2


def onehot(target, width):
    rows = target.shape[0]
    lanes = lax.broadcasted_iota(jnp.int32, (rows, width), 1)
    return jnp.where(lanes == target, 1.0, 0.0).astype(BF)


def rows_iota(rows):
    return lax.broadcasted_iota(jnp.int32, (rows, 1), 0)


def flip(c, x, last):
    return last * c + (1 - 2 * c) * x


def dot(a, b):
    return jnp.dot(a, b, preferred_element_type=F32)


def main_kernel(
    sizes,
    factor,
    nb_in,
    rot_in,
    cor_in,
    inp_in,
    cot_in,
    w_in,
    bias_in,
    out_o,
    ingrad_o,
    fin_o,
    out,
    ingrad,
    fin,
    nb,
    rot,
    cor,
    inp,
    w,
    bias,
    wt,
    pool,
    center,
    zl,
    zr,
    arr,
    terms,
    tst,
    spots,
    xs,
    cpad,
    wacc,
    wloc,
    core_in,
    p_out,
    p_in,
    z_all,
    s_load,
    s_store,
    s_edge,
    r_edge,
    s_term,
    r_term,
    s_core,
    r_core,
    s_p,
    r_p,
    s_z,
    r_z,
    s_g,
    r_g,
    s_last,
    r_last,
):
    nz, nx, ny = sizes
    count = nz * nx * ny * 2
    plane = nx * ny
    me = lax.axis_index("patch")
    here = inp.shape[0]
    loads = [
        pltpu.make_async_copy(src, dst, s_load.at[n])
        for n, (src, dst) in enumerate(
            [(inp_in, inp), (nb_in, nb), (rot_in, rot), (cor_in, cor)]
            + [(w_in, w), (bias_in, bias)]
            + [(cot_in.at[p], cpad.at[p, 4:36]) for p in range(here)]
        )
    ]
    for c in loads:
        c.start()
    core = lax.rem(me, 2)
    y = lax.rem(me // 2, ny)
    x = lax.rem(me // (2 * ny), nx)
    z = me // (2 * ny * nx)
    u, u_step = y + core * (z - y), 2 + core * (2 * plane - 2)
    v, v_step = z + core * (y - z), 2 * plane + core * (2 - 2 * plane)
    q = x * ny + u
    mate = me + 1 - 2 * core
    block = here * 4
    mr, tr = 1024 // (2 * plane), 128 // (2 * plane)

    def peer_of(k):
        xk, uk = lax.rem(x + k // ny, nx), lax.rem(u + lax.rem(k, ny), ny)
        return xk * ny + uk, me + 2 * ny * (xk - x) + u_step * (uk - u)

    def v_peer(k):
        return me + v_step * (lax.rem(v + k, nz) - v)

    def near(o):
        return lax.rem(me + o + count, count)

    def copy(src, dst, send, recv, to):
        return pltpu.make_async_remote_copy(
            src_ref=src,
            dst_ref=dst,
            send_sem=send,
            recv_sem=recv,
            device_id=(to,),
            device_id_type=MESH,
        )

    barrier = pltpu.get_barrier_semaphore()

    def greet(peer):
        pl.semaphore_signal(barrier, inc=1, device_id=(peer,), device_id_type=MESH)

    def greet_plane(k, carry):
        greet(peer_of(k)[1])
        return carry

    for k in range(1, nz):
        greet(v_peer(k))
    lax.fori_loop(1, plane, greet_plane, 0)
    for o in NEAR:
        greet(near(o))
    greet(mate)

    r64 = rows_iota(64)
    depth, along = r64 // 32, lax.rem(r64, 32)
    own = REACH * block
    loads[0].wait()

    def pack(p, carry):
        pool[own + p * 4] = inp[p, 0:2].reshape(64, 128)
        pool[own + p * 4 + 1] = inp[p, 30:32].reshape(64, 128)
        left = inp[p, :, 0:16, :].reshape(512, 128)
        pool[own + p * 4 + 2] = dot(onehot(along * 16 + depth, 512), left).astype(BF)
        right = inp[p, :, 16:32, :].reshape(512, 128)
        right = dot(onehot(along * 16 + depth + 14, 512), right)
        pool[own + p * 4 + 3] = right.astype(BF)
        return carry

    lax.fori_loop(0, here, pack, 0)
    pl.semaphore_wait(barrier, nz - 1 + plane - 1 + len(NEAR) + 1)
    edges = [
        copy(
            pool.at[pl.ds(own, block)],
            pool.at[pl.ds((REACH - o) * block, block)],
            s_edge.at[n],
            r_edge.at[n],
            near(o),
        )
        for n, o in enumerate(NEAR)
    ]
    for c in edges:
        c.start()
    for c in loads[1:]:
        c.wait()

    cols = lax.broadcasted_iota(jnp.int32, (32, 32, 128), 1)

    def middle(p, total):
        here_in = inp[p]
        wide = here_in.astype(F32)
        xs[p, 2:34, :, 128:256] = here_in
        ahead = jnp.where(cols >= 2, pltpu.roll(wide, 2, 1), 0.0)
        xs[p, 2:34, :, 0:128] = ahead.astype(BF)
        behind = jnp.where(cols < 30, pltpu.roll(wide, 30, 1), 0.0)
        xs[p, 2:34, :, 256:384] = behind.astype(BF)
        cpad[p, 0:4] = jnp.zeros((4, 32, 128), BF)
        cpad[p, 36:40] = jnp.zeros((4, 32, 128), BF)
        here_cot = cpad[p, 4:36]
        return total + here_cot.astype(F32).reshape(128, 8, 128).sum(axis=0)

    bias8 = lax.fori_loop(0, here, middle, jnp.zeros((8, 128), F32))
    bias_here = jnp.sum(bias8, axis=0, keepdims=True)
    wacc[...] = jnp.zeros_like(wacc)

    def outer_dot(a, b):
        return lax.dot_general(
            a, b, (((0,), (0,)), ((), ())), preferred_element_type=F32
        )

    def inner(n, carry):
        p, y0 = n // 4, lax.rem(n, 4) * 8 + 2
        lhs = xs[p, pl.ds(y0, 8)].reshape(256, 384)
        rhs = jnp.concatenate(
            [cpad[p, pl.ds(y0 + 4 - 2 * a, 8)].reshape(256, 128) for a in range(3)],
            axis=1,
        )
        wacc[...] += outer_dot(lhs, rhs)
        return carry

    lax.fori_loop(0, here * 4, inner, 0)

    for a in range(3):
        for b in range(3):
            piece = w[128 * (3 * a + b) : 128 * (3 * a + b) + 128]
            wt[128 * a : 128 * a + 128, 128 * b : 128 * b + 128] = piece.T
    cols6 = lax.broadcasted_iota(jnp.int32, (6, 32, 128), 1)

    def spread_back(n, carry):
        p, y0 = n // 6, lax.rem(n, 6) * 6
        lhs = jnp.concatenate(
            [cpad[p, pl.ds(y0 + 4 - 2 * a, 6)].reshape(192, 128) for a in range(3)],
            axis=1,
        )
        got = dot(lhs, wt[...])
        z0 = got[:, 0:128].reshape(6, 32, 128)
        z1 = got[:, 128:256].reshape(6, 32, 128)
        z2 = got[:, 256:384].reshape(6, 32, 128)
        zl[p, pl.ds(y0, 6)] = z0[:, 0:16].astype(BF)
        zr[p, pl.ds(y0, 6)] = z2[:, 16:32].astype(BF)
        total = z1 + jnp.where(cols6 < 30, pltpu.roll(z0, 30, 1), 0.0)
        total = total + jnp.where(cols6 >= 2, pltpu.roll(z2, 2, 1), 0.0)
        center[p, pl.ds(y0, 6)] = total
        return carry

    lax.fori_loop(0, here * 4, spread_back, 0)
    for c in edges:
        c.wait_recv()

    r192 = rows_iota(192)
    which, deep, on = r192 // 64, lax.rem(r192 // 32, 2), lax.rem(r192, 32)
    at = 2 * which + on
    r512 = rows_iota(512)
    line, place = r512 // 16, lax.rem(r512, 16)

    def halo(p, carry):
        def info(j):
            row, c1, c2 = side_scalars(j, nb[p, j], rot[p, j], me, count, here)
            return pool[row], c1, c2, cor[p, j] > 0

        for base, first in ((0, 0), (5, 34)):
            made = jnp.zeros((192, 128), F32)
            for j, c, inside in (
                (base, 30 + at, at < 2),
                (base + 1, at - 2, (at >= 2) & (at < 34)),
                (base + 2, at - 34, at >= 34),
            ):
                strip, c1, c2, present = info(j)
                target = 32 * flip(c1, deep, 1) + flip(c2, c, 31)
                target = jnp.where(inside & present, target, -1)
                made = made + dot(onehot(target, 64), strip)
            made = made.astype(BF)
            for b in range(3):
                piece = made[64 * b : 64 * b + 64].reshape(2, 32, 128)
                xs[p, first : first + 2, :, 128 * b : 128 * b + 128] = piece
        wacc[:, 0:128] += outer_dot(
            xs[p, 0:2].reshape(64, 384), cpad[p, 4:6].reshape(64, 128)
        )
        wacc[:, 256:384] += outer_dot(
            xs[p, 34:36].reshape(64, 384), cpad[p, 34:36].reshape(64, 128)
        )
        for j, shift, lo, lane in ((3, 0, 0, 0), (4, 14, 16, 256)):
            strip, c1, c2, present = info(j)
            side = place - shift
            target = 32 * flip(c1, side, 1) + flip(c2, line, 31)
            inside = (side >= 0) & (side < 2) & present
            made = dot(onehot(jnp.where(inside, target, -1), 64), strip)
            rhs = jnp.concatenate(
                [
                    cpad[p, 6 - 2 * a : 38 - 2 * a, lo : lo + 16].reshape(512, 128)
                    for a in range(3)
                ],
                axis=1,
            )
            wacc[lane : lane + 128] += outer_dot(made.astype(BF), rhs)
            old = xs[p, 2:34, lo : lo + 16, lane : lane + 128].astype(F32)
            xs[p, 2:34, lo : lo + 16, lane : lane + 128] = (
                old + made.reshape(32, 16, 128)
            ).astype(BF)
        return carry

    lax.fori_loop(0, here, halo, 0)

    wide = wloc.shape[1] - mr
    row_t = lax.broadcasted_iota(jnp.int32, (wide, 128), 0)

    def split_bias(tail):
        b = tail[tr : tr + 1] + tail[tr + 1 : tr + 2]
        top = b.astype(BF).astype(F32)
        return jnp.where(row_t == tr, top, jnp.where(row_t == tr + 1, b - top, tail))

    def tap(t):
        a, b = t // 3, t % 3
        return wacc[128 * b : 128 * b + 128, 128 * a : 128 * a + 128]

    each = 128 // mr
    for t in range(8):
        wloc[t * each : (t + 1) * each, 0:mr] = tap(t).reshape(each, mr, 128)
    last = tap(8)
    for s in range(2 * plane):
        rows = [last[s * tr : (s + 1) * tr], bias_here]
        rows.append(jnp.zeros((wide - tr - 1, 128), F32))
        wloc[s, mr:] = jnp.concatenate(rows, axis=0)

    swap = copy(
        wloc.at[pl.ds((1 - core) * plane, plane)], core_in, s_core, r_core, mate
    )
    swap.start()

    def conv(n, carry):
        p, i0 = n // 4, lax.rem(n, 4) * 8
        lhs = jnp.concatenate(
            [xs[p, pl.ds(i0 + 2 * a, 8)].reshape(256, 384) for a in range(3)], axis=1
        )
        out[p, pl.ds(i0, 8)] = (dot(lhs, w[...]) + bias[...]).astype(BF).reshape(8, 32, 128)
        return carry

    lax.fori_loop(here * 4, here * 5, spread_back, 0)
    swap.wait_recv()

    half = (nx // 2) * ny + ny // 2

    def order(n):
        return lax.rem(n // ny + nx // 2, nx) * ny + lax.rem(lax.rem(n, ny) + ny // 2, ny)

    def p_reduce(k):
        qk, peer = peer_of(k)
        return copy(p_out.at[qk], p_in.at[k - 1], s_p.at[k - 1], r_p.at[k - 1], peer)

    def every(fun, init):
        init = lax.fori_loop(0, half, lambda n, c: fun(order(n), c), init)
        return lax.fori_loop(half + 1, plane, lambda n, c: fun(order(n), c), init)

    def p_start(k, c):
        qk = peer_of(k)[0]
        slab = wloc[core * plane + qk] + core_in[qk]
        p_out[qk, 0:mr] = slab[0:mr].astype(BF)
        p_out[qk, mr:] = split_bias(slab[mr:]).astype(BF)
        p_reduce(k).start()
        return c

    every(p_start, 0)
    lax.fori_loop(here * 5, here * 6, spread_back, 0)

    def last_two(step, c):
        return jnp.where(c >= 30, step + c - 30, -1)

    def first_two(step, c):
        return jnp.where(c < 2, step + 14 + c, -1)

    def turn_back(p, carry):
        def back(j, target_of, piece):
            row, c1, c2 = side_scalars(j, nb[p, j], rot[p, j], me, count, here)
            target = target_of(flip(c1, depth, 1), flip(c2, along, 31))
            target = jnp.where(cor[p, j] > 0, target, -1)
            spots[p * 8 + j] = row
            tst[p * 8 + j] = dot(onehot(target, piece.shape[0]), piece)

        for base, lo in ((0, 0), (5, 34)):
            mid = center[p, lo : lo + 2].reshape(64, 128).astype(BF)
            ends = zl[p, lo : lo + 2].reshape(32, 128)
            back(base, lambda r, c: last_two(16 * r, c), ends)
            back(base + 1, lambda r, c: 32 * r + c, mid)
            ends = zr[p, lo : lo + 2].reshape(32, 128)
            back(base + 2, lambda r, c: first_two(16 * r, c), ends)
        back(3, lambda c, i: 16 * i + c, zl[p, 2:34].reshape(512, 128))
        back(4, lambda c, i: 16 * i + 14 + c, zr[p, 2:34].reshape(512, 128))
        return carry

    def gather_terms(s, carry):
        total = jnp.zeros((64, 128), F32)
        for n in range(here * 8):
            total = total + jnp.where(spots[n] == s, 1.0, 0.0) * tst[n]
        terms[s] = total.astype(BF)
        return carry

    lax.fori_loop(0, here, turn_back, 0)
    backs = []
    for n, o in enumerate(NEAR):
        first = (REACH + o) * block
        lax.fori_loop(first, first + block, gather_terms, 0)
        backs.append(
            copy(
                terms.at[pl.ds(first, block)],
                arr.at[n],
                s_term.at[n],
                r_term.at[n],
                near(o),
            )
        )
        backs[n].start()
    lax.fori_loop(own, own + block, gather_terms, 0)

    def p_add(k, c):
        p_reduce(k).wait_recv()
        return c + p_in[k - 1].astype(F32)

    z_all[v] = every(p_add, wloc[core * plane + q] + core_in[q])

    def z_gather(k):
        return copy(z_all.at[v], z_all.at[v], s_z.at[k - 1], r_z.at[k - 1], v_peer(k))

    for k in range(1, nz):
        z_gather(k).start()
    lax.fori_loop(0, 4 * here, conv, 0)
    stores = [pltpu.make_async_copy(out, out_o, s_store.at[0])]
    stores[0].start()
    for k in range(1, nz):
        z_gather(k).wait_recv()
    slab = z_all[0]
    for n in range(1, nz):
        slab = slab + z_all[n]
    slab = slab * factor
    spot = core * plane + q
    fin[spot, 0:mr] = slab[0:mr].astype(BF)
    fin[spot, mr:] = split_bias(slab[mr:]).astype(BF)

    def p_gather(k):
        return copy(fin.at[spot], fin.at[spot], s_g.at[k - 1], r_g.at[k - 1], peer_of(k)[1])

    def g_start(k, c):
        p_gather(k).start()
        return c

    every(g_start, 0)
    for c in backs:
        c.wait_recv()

    def finish(p, carry):
        def pieces_of(slot):
            found = [terms[REACH * block + p * 4 + slot]]
            return found + [arr[n, p * 4 + slot] for n in range(len(NEAR))]

        def arrived(slot):
            total = jnp.zeros((64, 128), F32)
            for piece in pieces_of(slot):
                total = total + piece.astype(F32)
            return total.reshape(2, 32, 128)

        top, bottom = arrived(0), arrived(1)
        for slot, shift, lo in ((2, 0, 0), (3, 14, 16)):
            at_col = place - shift
            inside = (at_col >= 0) & (at_col < 2)
            spread = onehot(jnp.where(inside, 32 * at_col + line, -1), 64)
            made = jnp.zeros((512, 128), F32)
            for piece in pieces_of(slot):
                made = made + dot(spread, piece)
            total = center[p, 2:34, lo : lo + 16] + made.reshape(32, 16, 128)
            upper = total[0:2] + top[:, lo : lo + 16]
            lower = total[30:32] + bottom[:, lo : lo + 16]
            ingrad[p, 0:2, lo : lo + 16] = upper.astype(BF)
            ingrad[p, 2:30, lo : lo + 16] = total[2:30].astype(BF)
            ingrad[p, 30:32, lo : lo + 16] = lower.astype(BF)
        return carry

    lax.fori_loop(0, here, finish, 0)
    stores.append(pltpu.make_async_copy(ingrad, ingrad_o, s_store.at[1]))
    stores[1].start()

    def g_wait(k, c):
        p_gather(k).wait_recv()
        return c

    every(g_wait, 0)
    mine = pl.ds(core * plane, plane)
    hand = copy(fin.at[mine], fin_o.at[mine], s_last, r_last, mate)
    hand.start()
    stores.append(pltpu.make_async_copy(fin.at[mine], fin_o.at[mine], s_store.at[2]))
    stores[2].start()

    def sent(k, c):
        p_reduce(k).wait_send()
        p_gather(k).wait_send()
        return c

    every(sent, 0)
    for c in edges + backs + [swap]:
        c.wait_send()
    for k in range(1, nz):
        z_gather(k).wait_send()
    for c in stores:
        c.wait()
    hand.wait()


def write_kernel(
    mr, tr, out, ingrad, fin_o, out_o, ingrad_o, wgrad_o, bgrad, fin, held, wide, sems
):
    here = out.shape[0]
    load = pltpu.make_async_copy(fin_o, fin, sems.at[0])
    load.start()
    loads, stores = [], []
    for p in range(here):
        for n, (src, dst) in enumerate(((out, out_o), (ingrad, ingrad_o))):
            at = 2 * p + n
            loads.append(
                pltpu.make_async_copy(src.at[p], held.at[at], sems.at[2 + 2 * at])
            )
            stores.append(
                pltpu.make_async_copy(held.at[at], dst.at[p], sems.at[3 + 2 * at])
            )
            loads[-1].start()
    for c, d in zip(loads, stores):
        c.wait()
        d.start()
    load.wait()
    slabs = fin.shape[0]
    wide[0:1024] = fin[:, 0:mr].astype(F32).reshape(1024, 128)
    for s in range(slabs):
        tail = fin[s, mr:].astype(F32)
        wide[1024 + tr * s : 1024 + tr * (s + 1)] = tail[0:tr]
    stores.append(pltpu.make_async_copy(wide, wgrad_o, sems.at[1]))
    stores[-1].start()
    tail = fin[0, mr:].astype(F32)
    bgrad[...] = tail[tr : tr + 1] + tail[tr + 1 : tr + 2]
    for c in stores:
        c.wait()


def body(count, inputs, cotangent, weights, bias_vector, neighbours, rotations, corners):
    here, length, _, chans = inputs.shape
    sizes = TORUS[count]
    nz, nx, ny = sizes
    plane = nx * ny
    factor = 1.0 / (length * math.sqrt(here * count))
    block = here * 4
    hbm = pl.BlockSpec(memory_space=pltpu.HBM)
    vmem = pl.BlockSpec(memory_space=pltpu.VMEM)
    dma = pltpu.SemaphoreType.DMA
    mr, tr = 1024 // (2 * plane), 128 // (2 * plane)
    rows = mr + -(-(tr + 2) // 8) * 8
    near = len(NEAR)
    wires = [near, near, None, plane - 1, nz - 1, plane - 1, None]
    outputs, input_grad, fin = pl.pallas_call(
        functools.partial(main_kernel, sizes, factor),
        out_shape=(
            jax.ShapeDtypeStruct(inputs.shape, BF),
            jax.ShapeDtypeStruct(inputs.shape, BF),
            jax.ShapeDtypeStruct((2 * plane, rows, chans), BF),
        ),
        in_specs=[hbm] * 7,
        out_specs=(hbm,) * 3,
        scratch_shapes=[
            pltpu.VMEM(inputs.shape, BF),
            pltpu.VMEM(inputs.shape, BF),
            pltpu.VMEM((2 * plane, rows, chans), BF),
            pltpu.SMEM((here, 8), jnp.int32),
            pltpu.SMEM((here, 8), jnp.int32),
            pltpu.SMEM((here, 8), jnp.int32),
            pltpu.VMEM(inputs.shape, BF),
            pltpu.VMEM((9 * chans, chans), BF),
            pltpu.VMEM((1, chans), F32),
            pltpu.VMEM((3 * chans, 3 * chans), BF),
            pltpu.VMEM((5 * block, 64, chans), BF),
            pltpu.VMEM((here, 36, 32, chans), F32),
            pltpu.VMEM((here, 36, 16, chans), BF),
            pltpu.VMEM((here, 36, 16, chans), BF),
            pltpu.VMEM((near, block, 64, chans), BF),
            pltpu.VMEM((5 * block, 64, chans), BF),
            pltpu.VMEM((here * 8, 64, chans), F32),
            pltpu.SMEM((here * 8,), jnp.int32),
            pltpu.VMEM((here, 36, 32, 3 * chans), BF),
            pltpu.VMEM((here, 40, 32, chans), BF),
            pltpu.VMEM((3 * chans, 3 * chans), F32),
            pltpu.VMEM((2 * plane, rows, chans), F32),
            pltpu.VMEM((plane, rows, chans), F32),
            pltpu.VMEM((plane, rows, chans), BF),
            pltpu.VMEM((plane - 1, rows, chans), BF),
            pltpu.VMEM((nz, rows, chans), F32),
            dma((6 + here,)),
            dma((3,)),
        ]
        + [dma if n is None else dma((n,)) for n in wires for _ in range(2)],
        compiler_params=pltpu.CompilerParams(
            collective_id=0, has_side_effects=True, vmem_limit_bytes=56 * 2**20
        ),
    )(
        neighbours,
        rotations,
        corners,
        inputs,
        cotangent,
        weights.reshape(9 * chans, chans),
        bias_vector.reshape(1, chans),
    )
    outputs, input_grad, weight_grad, bias_grad = pl.pallas_call(
        functools.partial(write_kernel, mr, tr),
        out_shape=(
            jax.ShapeDtypeStruct(inputs.shape, BF),
            jax.ShapeDtypeStruct(inputs.shape, BF),
            jax.ShapeDtypeStruct((9 * chans, chans), F32),
            jax.ShapeDtypeStruct((1, chans), F32),
        ),
        in_specs=[hbm] * 3,
        out_specs=(hbm, hbm, hbm, vmem),
        scratch_shapes=[
            pltpu.VMEM((2 * plane, rows, chans), BF),
            pltpu.VMEM((2 * here, length, length, chans), BF),
            pltpu.VMEM((9 * chans, chans), F32),
            dma((2 + 4 * here,)),
        ],
        compiler_params=pltpu.CompilerParams(vmem_limit_bytes=56 * 2**20),
    )(outputs, input_grad, fin)
    return (
        outputs,
        input_grad,
        weight_grad.reshape(weights.shape),
        bias_grad.reshape(bias_vector.shape),
    )


def solution(mesh):
    in_specs = (
        P("patch", None, None, None),
        P("patch", None, None, None),
        P(),
        P(),
        P("patch", None),
        P("patch", None),
        P("patch", None),
    )
    out_specs = (P("patch", None, None, None), P("patch", None, None, None), P(), P())
    return jax.shard_map(
        functools.partial(body, mesh.shape["patch"]),
        mesh=mesh,
        in_specs=in_specs,
        out_specs=out_specs,
        check_vma=False,
    )
```

```python
import functools
import math

import jax
import jax.numpy as jnp
from jax import lax
from jax.experimental import pallas as pl
from jax.experimental.pallas import tpu as pltpu
from jax.sharding import PartitionSpec as P

REACH = 2
NEAR = (-2, 2, -1, 1)
MESH = pl.DeviceIdType.MESH
BF = jnp.bfloat16
F32 = jnp.float32
SIDE_TABLE = (
    ((0, 0), (3, 1), (1, 3), (2, 2)),
    ((1, 0), (2, 1), (0, 3), (3, 2)),
    ((2, 0), (0, 2), (3, 3), (1, 1)),
    ((3, 0), (1, 2), (2, 3), (0, 1)),
)
WANTED = (1, 1, 1, 3, 2, 0, 0, 0)
TORUS = {512: (8, 4, 8), 16: (2, 2, 2)}


def pick(k, values):
    out = jnp.int32(values[3])
    for i in (2, 1, 0):
        out = jnp.where(k == i, jnp.int32(values[i]), out)
    return out


def side_scalars(j, nb, rot, me, count, here):
    owner = nb // here
    off = lax.rem(owner - me + REACH + count, count)
    place = jnp.minimum(off, 2 * REACH) * here + (nb - owner * here)
    table = SIDE_TABLE[WANTED[j]]
    slot = pick(rot, [table[k][0] for k in range(4)])
    c1 = pick(rot, [table[k][1] & 1 for k in range(4)])
    c2 = pick(rot, [table[k][1] >> 1 for k in range(4)])
    return place * 4 + slot, c1, c2


def onehot(target, width):
    rows = target.shape[0]
    lanes = lax.broadcasted_iota(jnp.int32, (rows, width), 1)
    return jnp.where(lanes == target, 1.0, 0.0).astype(BF)


def rows_iota(rows):
    return lax.broadcasted_iota(jnp.int32, (rows, 1), 0)


def flip(c, x, last):
    return last * c + (1 - 2 * c) * x


def dot(a, b):
    return jnp.dot(a, b, preferred_element_type=F32)


def main_kernel(
    sizes,
    factor,
    nb_in,
    rot_in,
    cor_in,
    inp_in,
    cot_in,
    w_in,
    bias_in,
    out_o,
    ingrad_o,
    fin_o,
    out,
    ingrad,
    fin,
    nb,
    rot,
    cor,
    inp,
    w,
    bias,
    wt,
    pool,
    center,
    zl,
    zr,
    arr,
    terms,
    tst,
    spots,
    xs,
    cpad,
    wacc,
    wloc,
    core_in,
    p_out,
    p_in,
    z_all,
    s_load,
    s_store,
    s_edge,
    r_edge,
    s_term,
    r_term,
    s_core,
    r_core,
    s_p,
    r_p,
    s_z,
    r_z,
    s_g,
    r_g,
    s_last,
    r_last,
):
    nz, nx, ny = sizes
    count = nz * nx * ny * 2
    plane = nx * ny
    me = lax.axis_index("patch")
    here = inp.shape[0]
    loads = [
        pltpu.make_async_copy(src, dst, s_load.at[n])
        for n, (src, dst) in enumerate(
            [(inp_in, inp), (nb_in, nb), (rot_in, rot), (cor_in, cor)]
            + [(w_in, w), (bias_in, bias)]
            + [(cot_in.at[p], cpad.at[p, 4:36]) for p in range(here)]
        )
    ]
    for c in loads:
        c.start()
    core = lax.rem(me, 2)
    y = lax.rem(me // 2, ny)
    x = lax.rem(me // (2 * ny), nx)
    z = me // (2 * ny * nx)
    u, u_step = y + core * (z - y), 2 + core * (2 * plane - 2)
    v, v_step = z + core * (y - z), 2 * plane + core * (2 - 2 * plane)
    q = x * ny + u
    mate = me + 1 - 2 * core
    block = here * 4
    mr, tr = 1024 // (2 * plane), 128 // (2 * plane)

    def peer_of(k):
        xk, uk = lax.rem(x + k // ny, nx), lax.rem(u + lax.rem(k, ny), ny)
        return xk * ny + uk, me + 2 * ny * (xk - x) + u_step * (uk - u)

    def v_peer(k):
        return me + v_step * (lax.rem(v + k, nz) - v)

    def near(o):
        return lax.rem(me + o + count, count)

    def copy(src, dst, send, recv, to):
        return pltpu.make_async_remote_copy(
            src_ref=src,
            dst_ref=dst,
            send_sem=send,
            recv_sem=recv,
            device_id=(to,),
            device_id_type=MESH,
        )

    barrier = pltpu.get_barrier_semaphore()

    def greet(peer):
        pl.semaphore_signal(barrier, inc=1, device_id=(peer,), device_id_type=MESH)

    def greet_plane(k, carry):
        greet(peer_of(k)[1])
        return carry

    for k in range(1, nz):
        greet(v_peer(k))
    lax.fori_loop(1, plane, greet_plane, 0)
    for o in NEAR:
        greet(near(o))
    greet(mate)

    r64 = rows_iota(64)
    depth, along = r64 // 32, lax.rem(r64, 32)
    own = REACH * block
    loads[0].wait()

    def pack(p, carry):
        pool[own + p * 4] = inp[p, 0:2].reshape(64, 128)
        pool[own + p * 4 + 1] = inp[p, 30:32].reshape(64, 128)
        left = inp[p, :, 0:16, :].reshape(512, 128)
        pool[own + p * 4 + 2] = dot(onehot(along * 16 + depth, 512), left).astype(BF)
        right = inp[p, :, 16:32, :].reshape(512, 128)
        right = dot(onehot(along * 16 + depth + 14, 512), right)
        pool[own + p * 4 + 3] = right.astype(BF)
        return carry

    lax.fori_loop(0, here, pack, 0)
    pl.semaphore_wait(barrier, nz - 1 + plane - 1 + len(NEAR) + 1)
    edges = [
        copy(
            pool.at[pl.ds(own, block)],
            pool.at[pl.ds((REACH - o) * block, block)],
            s_edge.at[n],
            r_edge.at[n],
            near(o),
        )
        for n, o in enumerate(NEAR)
    ]
    for c in edges:
        c.start()
    for c in loads[1:]:
        c.wait()

    cols = lax.broadcasted_iota(jnp.int32, (32, 32, 128), 1)

    def middle(p, total):
        here_in = inp[p]
        wide = here_in.astype(F32)
        xs[p, 2:34, :, 128:256] = here_in
        ahead = jnp.where(cols >= 2, pltpu.roll(wide, 2, 1), 0.0)
        xs[p, 2:34, :, 0:128] = ahead.astype(BF)
        behind = jnp.where(cols < 30, pltpu.roll(wide, 30, 1), 0.0)
        xs[p, 2:34, :, 256:384] = behind.astype(BF)
        cpad[p, 0:4] = jnp.zeros((4, 32, 128), BF)
        cpad[p, 36:40] = jnp.zeros((4, 32, 128), BF)
        here_cot = cpad[p, 4:36]
        return total + here_cot.astype(F32).reshape(128, 8, 128).sum(axis=0)

    bias8 = lax.fori_loop(0, here, middle, jnp.zeros((8, 128), F32))
    bias_here = jnp.sum(bias8, axis=0, keepdims=True)
    wacc[...] = jnp.zeros_like(wacc)

    def outer_dot(a, b):
        return lax.dot_general(
            a, b, (((0,), (0,)), ((), ())), preferred_element_type=F32
        )

    def inner(n, carry):
        p, y0 = n // 4, lax.rem(n, 4) * 8 + 2
        lhs = xs[p, pl.ds(y0, 8)].reshape(256, 384)
        rhs = jnp.concatenate(
            [cpad[p, pl.ds(y0 + 4 - 2 * a, 8)].reshape(256, 128) for a in range(3)],
            axis=1,
        )
        wacc[...] += outer_dot(lhs, rhs)
        return carry

    lax.fori_loop(0, here * 4, inner, 0)

    for a in range(3):
        for b in range(3):
            piece = w[128 * (3 * a + b) : 128 * (3 * a + b) + 128]
            wt[128 * a : 128 * a + 128, 128 * b : 128 * b + 128] = piece.T
    cols6 = lax.broadcasted_iota(jnp.int32, (6, 32, 128), 1)

    def spread_back(n, carry):
        p, y0 = n // 6, lax.rem(n, 6) * 6
        lhs = jnp.concatenate(
            [cpad[p, pl.ds(y0 + 4 - 2 * a, 6)].reshape(192, 128) for a in range(3)],
            axis=1,
        )
        got = dot(lhs, wt[...])
        z0 = got[:, 0:128].reshape(6, 32, 128)
        z1 = got[:, 128:256].reshape(6, 32, 128)
        z2 = got[:, 256:384].reshape(6, 32, 128)
        zl[p, pl.ds(y0, 6)] = z0[:, 0:16].astype(BF)
        zr[p, pl.ds(y0, 6)] = z2[:, 16:32].astype(BF)
        total = z1 + jnp.where(cols6 < 30, pltpu.roll(z0, 30, 1), 0.0)
        total = total + jnp.where(cols6 >= 2, pltpu.roll(z2, 2, 1), 0.0)
        center[p, pl.ds(y0, 6)] = total
        return carry

    lax.fori_loop(0, here * 4, spread_back, 0)
    for c in edges:
        c.wait_recv()

    r192 = rows_iota(192)
    which, deep, on = r192 // 64, lax.rem(r192 // 32, 2), lax.rem(r192, 32)
    at = 2 * which + on
    r512 = rows_iota(512)
    line, place = r512 // 16, lax.rem(r512, 16)

    def halo(p, carry):
        def info(j):
            row, c1, c2 = side_scalars(j, nb[p, j], rot[p, j], me, count, here)
            return pool[row], c1, c2, cor[p, j] > 0

        for base, first in ((0, 0), (5, 34)):
            made = jnp.zeros((192, 128), F32)
            for j, c, inside in (
                (base, 30 + at, at < 2),
                (base + 1, at - 2, (at >= 2) & (at < 34)),
                (base + 2, at - 34, at >= 34),
            ):
                strip, c1, c2, present = info(j)
                target = 32 * flip(c1, deep, 1) + flip(c2, c, 31)
                target = jnp.where(inside & present, target, -1)
                made = made + dot(onehot(target, 64), strip)
            made = made.astype(BF)
            for b in range(3):
                piece = made[64 * b : 64 * b + 64].reshape(2, 32, 128)
                xs[p, first : first + 2, :, 128 * b : 128 * b + 128] = piece
        wacc[:, 0:128] += outer_dot(
            xs[p, 0:2].reshape(64, 384), cpad[p, 4:6].reshape(64, 128)
        )
        wacc[:, 256:384] += outer_dot(
            xs[p, 34:36].reshape(64, 384), cpad[p, 34:36].reshape(64, 128)
        )
        for j, shift, lo, lane in ((3, 0, 0, 0), (4, 14, 16, 256)):
            strip, c1, c2, present = info(j)
            side = place - shift
            target = 32 * flip(c1, side, 1) + flip(c2, line, 31)
            inside = (side >= 0) & (side < 2) & present
            made = dot(onehot(jnp.where(inside, target, -1), 64), strip)
            rhs = jnp.concatenate(
                [
                    cpad[p, 6 - 2 * a : 38 - 2 * a, lo : lo + 16].reshape(512, 128)
                    for a in range(3)
                ],
                axis=1,
            )
            wacc[lane : lane + 128] += outer_dot(made.astype(BF), rhs)
            old = xs[p, 2:34, lo : lo + 16, lane : lane + 128].astype(F32)
            xs[p, 2:34, lo : lo + 16, lane : lane + 128] = (
                old + made.reshape(32, 16, 128)
            ).astype(BF)
        return carry

    lax.fori_loop(0, here, halo, 0)

    wide = wloc.shape[1] - mr
    row_t = lax.broadcasted_iota(jnp.int32, (wide, 128), 0)

    def split_bias(tail):
        b = tail[tr : tr + 1] + tail[tr + 1 : tr + 2]
        top = b.astype(BF).astype(F32)
        return jnp.where(row_t == tr, top, jnp.where(row_t == tr + 1, b - top, tail))

    def tap(t):
        a, b = t // 3, t % 3
        return wacc[128 * b : 128 * b + 128, 128 * a : 128 * a + 128]

    each = 128 // mr
    for t in range(8):
        wloc[t * each : (t + 1) * each, 0:mr] = tap(t).reshape(each, mr, 128)
    last = tap(8)
    for s in range(2 * plane):
        rows = [last[s * tr : (s + 1) * tr], bias_here]
        rows.append(jnp.zeros((wide - tr - 1, 128), F32))
        wloc[s, mr:] = jnp.concatenate(rows, axis=0)

    swap = copy(
        wloc.at[pl.ds((1 - core) * plane, plane)], core_in, s_core, r_core, mate
    )
    swap.start()

    def conv(n, carry):
        p, i0 = n // 4, lax.rem(n, 4) * 8
        lhs = jnp.concatenate(
            [xs[p, pl.ds(i0 + 2 * a, 8)].reshape(256, 384) for a in range(3)], axis=1
        )
        out[p, pl.ds(i0, 8)] = (dot(lhs, w[...]) + bias[...]).astype(BF).reshape(8, 32, 128)
        return carry

    lax.fori_loop(here * 4, here * 6, spread_back, 0)
    swap.wait_recv()

    half = (nx // 2) * ny + ny // 2

    def order(n):
        return lax.rem(n // ny + nx // 2, nx) * ny + lax.rem(lax.rem(n, ny) + ny // 2, ny)

    def p_reduce(k):
        qk, peer = peer_of(k)
        return copy(p_out.at[qk], p_in.at[k - 1], s_p.at[k - 1], r_p.at[k - 1], peer)

    def every(fun, init):
        init = lax.fori_loop(0, half, lambda n, c: fun(order(n), c), init)
        return lax.fori_loop(half + 1, plane, lambda n, c: fun(order(n), c), init)

    def p_start(k, c):
        qk = peer_of(k)[0]
        slab = wloc[core * plane + qk] + core_in[qk]
        p_out[qk, 0:mr] = slab[0:mr].astype(BF)
        p_out[qk, mr:] = split_bias(slab[mr:]).astype(BF)
        p_reduce(k).start()
        return c

    every(p_start, 0)

    def last_two(step, c):
        return jnp.where(c >= 30, step + c - 30, -1)

    def first_two(step, c):
        return jnp.where(c < 2, step + 14 + c, -1)

    def turn_back(p, carry):
        def back(j, target_of, piece):
            row, c1, c2 = side_scalars(j, nb[p, j], rot[p, j], me, count, here)
            target = target_of(flip(c1, depth, 1), flip(c2, along, 31))
            target = jnp.where(cor[p, j] > 0, target, -1)
            spots[p * 8 + j] = row
            tst[p * 8 + j] = dot(onehot(target, piece.shape[0]), piece)

        for base, lo in ((0, 0), (5, 34)):
            mid = center[p, lo : lo + 2].reshape(64, 128).astype(BF)
            ends = zl[p, lo : lo + 2].reshape(32, 128)
            back(base, lambda r, c: last_two(16 * r, c), ends)
            back(base + 1, lambda r, c: 32 * r + c, mid)
            ends = zr[p, lo : lo + 2].reshape(32, 128)
            back(base + 2, lambda r, c: first_two(16 * r, c), ends)
        back(3, lambda c, i: 16 * i + c, zl[p, 2:34].reshape(512, 128))
        back(4, lambda c, i: 16 * i + 14 + c, zr[p, 2:34].reshape(512, 128))
        return carry

    def gather_terms(s, carry):
        total = jnp.zeros((64, 128), F32)
        for n in range(here * 8):
            total = total + jnp.where(spots[n] == s, 1.0, 0.0) * tst[n]
        terms[s] = total.astype(BF)
        return carry

    lax.fori_loop(0, here, turn_back, 0)
    backs = []
    for n, o in enumerate(NEAR):
        first = (REACH + o) * block
        lax.fori_loop(first, first + block, gather_terms, 0)
        backs.append(
            copy(
                terms.at[pl.ds(first, block)],
                arr.at[n],
                s_term.at[n],
                r_term.at[n],
                near(o),
            )
        )
        backs[n].start()
    lax.fori_loop(own, own + block, gather_terms, 0)

    def p_add(k, c):
        p_reduce(k).wait_recv()
        return c + p_in[k - 1].astype(F32)

    z_all[v] = every(p_add, wloc[core * plane + q] + core_in[q])

    def z_gather(k):
        return copy(z_all.at[v], z_all.at[v], s_z.at[k - 1], r_z.at[k - 1], v_peer(k))

    for k in range(1, nz):
        z_gather(k).start()
    lax.fori_loop(0, 4 * here, conv, 0)
    stores = [pltpu.make_async_copy(out, out_o, s_store.at[0])]
    stores[0].start()
    for k in range(1, nz):
        z_gather(k).wait_recv()
    slab = z_all[0]
    for n in range(1, nz):
        slab = slab + z_all[n]
    slab = slab * factor
    spot = core * plane + q
    fin[spot, 0:mr] = slab[0:mr].astype(BF)
    fin[spot, mr:] = split_bias(slab[mr:]).astype(BF)

    def p_gather(k):
        return copy(fin.at[spot], fin.at[spot], s_g.at[k - 1], r_g.at[k - 1], peer_of(k)[1])

    def g_start(k, c):
        p_gather(k).start()
        return c

    every(g_start, 0)
    for c in backs:
        c.wait_recv()

    def finish(p, carry):
        def pieces_of(slot):
            found = [terms[REACH * block + p * 4 + slot]]
            return found + [arr[n, p * 4 + slot] for n in range(len(NEAR))]

        def arrived(slot):
            total = jnp.zeros((64, 128), F32)
            for piece in pieces_of(slot):
                total = total + piece.astype(F32)
            return total.reshape(2, 32, 128)

        top, bottom = arrived(0), arrived(1)
        for slot, shift, lo in ((2, 0, 0), (3, 14, 16)):
            at_col = place - shift
            inside = (at_col >= 0) & (at_col < 2)
            spread = onehot(jnp.where(inside, 32 * at_col + line, -1), 64)
            made = jnp.zeros((512, 128), F32)
            for piece in pieces_of(slot):
                made = made + dot(spread, piece)
            total = center[p, 2:34, lo : lo + 16] + made.reshape(32, 16, 128)
            upper = total[0:2] + top[:, lo : lo + 16]
            lower = total[30:32] + bottom[:, lo : lo + 16]
            ingrad[p, 0:2, lo : lo + 16] = upper.astype(BF)
            ingrad[p, 2:30, lo : lo + 16] = total[2:30].astype(BF)
            ingrad[p, 30:32, lo : lo + 16] = lower.astype(BF)
        return carry

    lax.fori_loop(0, here, finish, 0)
    stores.append(pltpu.make_async_copy(ingrad, ingrad_o, s_store.at[1]))
    stores[1].start()

    def g_wait(k, c):
        p_gather(k).wait_recv()
        return c

    every(g_wait, 0)
    mine = pl.ds(core * plane, plane)
    hand = copy(fin.at[mine], fin_o.at[mine], s_last, r_last, mate)
    hand.start()
    stores.append(pltpu.make_async_copy(fin.at[mine], fin_o.at[mine], s_store.at[2]))
    stores[2].start()

    def sent(k, c):
        p_reduce(k).wait_send()
        p_gather(k).wait_send()
        return c

    every(sent, 0)
    for c in edges + backs + [swap]:
        c.wait_send()
    for k in range(1, nz):
        z_gather(k).wait_send()
    for c in stores:
        c.wait()
    hand.wait()


def write_kernel(
    mr, tr, out, ingrad, fin_o, out_o, ingrad_o, wgrad_o, bgrad, fin, held, wide, sems
):
    here = out.shape[0]
    load = pltpu.make_async_copy(fin_o, fin, sems.at[0])
    load.start()
    loads, stores = [], []
    for p in range(here):
        for n, (src, dst) in enumerate(((out, out_o), (ingrad, ingrad_o))):
            at = 2 * p + n
            loads.append(
                pltpu.make_async_copy(src.at[p], held.at[at], sems.at[2 + 2 * at])
            )
            stores.append(
                pltpu.make_async_copy(held.at[at], dst.at[p], sems.at[3 + 2 * at])
            )
            loads[-1].start()
    for c, d in zip(loads, stores):
        c.wait()
        d.start()
    load.wait()
    slabs = fin.shape[0]
    wide[0:1024] = fin[:, 0:mr].astype(F32).reshape(1024, 128)
    for s in range(slabs):
        tail = fin[s, mr:].astype(F32)
        wide[1024 + tr * s : 1024 + tr * (s + 1)] = tail[0:tr]
    stores.append(pltpu.make_async_copy(wide, wgrad_o, sems.at[1]))
    stores[-1].start()
    tail = fin[0, mr:].astype(F32)
    bgrad[...] = tail[tr : tr + 1] + tail[tr + 1 : tr + 2]
    for c in stores:
        c.wait()


def body(count, inputs, cotangent, weights, bias_vector, neighbours, rotations, corners):
    here, length, _, chans = inputs.shape
    sizes = TORUS[count]
    nz, nx, ny = sizes
    plane = nx * ny
    factor = 1.0 / (length * math.sqrt(here * count))
    block = here * 4
    hbm = pl.BlockSpec(memory_space=pltpu.HBM)
    vmem = pl.BlockSpec(memory_space=pltpu.VMEM)
    dma = pltpu.SemaphoreType.DMA
    mr, tr = 1024 // (2 * plane), 128 // (2 * plane)
    rows = mr + -(-(tr + 2) // 8) * 8
    near = len(NEAR)
    wires = [near, near, None, plane - 1, nz - 1, plane - 1, None]
    outputs, input_grad, fin = pl.pallas_call(
        functools.partial(main_kernel, sizes, factor),
        out_shape=(
            jax.ShapeDtypeStruct(inputs.shape, BF),
            jax.ShapeDtypeStruct(inputs.shape, BF),
            jax.ShapeDtypeStruct((2 * plane, rows, chans), BF),
        ),
        in_specs=[hbm] * 7,
        out_specs=(hbm,) * 3,
        scratch_shapes=[
            pltpu.VMEM(inputs.shape, BF),
            pltpu.VMEM(inputs.shape, BF),
            pltpu.VMEM((2 * plane, rows, chans), BF),
            pltpu.SMEM((here, 8), jnp.int32),
            pltpu.SMEM((here, 8), jnp.int32),
            pltpu.SMEM((here, 8), jnp.int32),
            pltpu.VMEM(inputs.shape, BF),
            pltpu.VMEM((9 * chans, chans), BF),
            pltpu.VMEM((1, chans), F32),
            pltpu.VMEM((3 * chans, 3 * chans), BF),
            pltpu.VMEM((5 * block, 64, chans), BF),
            pltpu.VMEM((here, 36, 32, chans), F32),
            pltpu.VMEM((here, 36, 16, chans), BF),
            pltpu.VMEM((here, 36, 16, chans), BF),
            pltpu.VMEM((near, block, 64, chans), BF),
            pltpu.VMEM((5 * block, 64, chans), BF),
            pltpu.VMEM((here * 8, 64, chans), F32),
            pltpu.SMEM((here * 8,), jnp.int32),
            pltpu.VMEM((here, 36, 32, 3 * chans), BF),
            pltpu.VMEM((here, 40, 32, chans), BF),
            pltpu.VMEM((3 * chans, 3 * chans), F32),
            pltpu.VMEM((2 * plane, rows, chans), F32),
            pltpu.VMEM((plane, rows, chans), F32),
            pltpu.VMEM((plane, rows, chans), BF),
            pltpu.VMEM((plane - 1, rows, chans), BF),
            pltpu.VMEM((nz, rows, chans), F32),
            dma((6 + here,)),
            dma((3,)),
        ]
        + [dma if n is None else dma((n,)) for n in wires for _ in range(2)],
        compiler_params=pltpu.CompilerParams(
            collective_id=0, has_side_effects=True, vmem_limit_bytes=56 * 2**20
        ),
    )(
        neighbours,
        rotations,
        corners,
        inputs,
        cotangent,
        weights.reshape(9 * chans, chans),
        bias_vector.reshape(1, chans),
    )
    outputs, input_grad, weight_grad, bias_grad = pl.pallas_call(
        functools.partial(write_kernel, mr, tr),
        out_shape=(
            jax.ShapeDtypeStruct(inputs.shape, BF),
            jax.ShapeDtypeStruct(inputs.shape, BF),
            jax.ShapeDtypeStruct((9 * chans, chans), F32),
            jax.ShapeDtypeStruct((1, chans), F32),
        ),
        in_specs=[hbm] * 3,
        out_specs=(hbm, hbm, hbm, vmem),
        scratch_shapes=[
            pltpu.VMEM((2 * plane, rows, chans), BF),
            pltpu.VMEM((2 * here, length, length, chans), BF),
            pltpu.VMEM((9 * chans, chans), F32),
            dma((2 + 4 * here,)),
        ],
        compiler_params=pltpu.CompilerParams(vmem_limit_bytes=56 * 2**20),
    )(outputs, input_grad, fin)
    return (
        outputs,
        input_grad,
        weight_grad.reshape(weights.shape),
        bias_grad.reshape(bias_vector.shape),
    )


def solution(mesh):
    in_specs = (
        P("patch", None, None, None),
        P("patch", None, None, None),
        P(),
        P(),
        P("patch", None),
        P("patch", None),
        P("patch", None),
    )
    out_specs = (P("patch", None, None, None), P("patch", None, None, None), P(), P())
    return jax.shard_map(
        functools.partial(body, mesh.shape["patch"]),
        mesh=mesh,
        in_specs=in_specs,
        out_specs=out_specs,
        check_vma=False,
    )
```
